256 devices in a mesh: dp: 16 (over y, x_lo, core), tensor: 16 (over z, x_hi).
Axes of the slice: x: 4 (x_hi: 2, x_lo: 2; x = x_hi * 2 + x_lo), y: 4, z: 8, core: 2. Of those that a mesh axis runs over, the one named last changes fastest.
Arguments:
- in_one: bfloat16 [65536, 5120], P('dp', 'tensor'), may hold values from -6 to 6
- grad_one: bfloat16 [65536, 5120], P('dp', 'tensor'), may hold values from -6 to 6
- in_two: bfloat16 [65536, 5120], P('dp', 'tensor'), may hold values from -6 to 6
- grad_two: bfloat16 [65536, 5120], P('dp', 'tensor'), may hold values from -6 to 6
- proj_in_one: bfloat16 [5120, 64], P('tensor'), may hold values from -0.078125 to 0.078125
- proj_out_one: bfloat16 [5120, 64], P('tensor'), may hold values from -0.078125 to 0.078125
- proj_in_two: bfloat16 [5120, 64], P('tensor'), may hold values from -0.078125 to 0.078125
- proj_out_two: bfloat16 [5120, 64], P('tensor'), may hold values from -0.078125 to 0.078125
- query_index: int32 [64], replicated, may hold values from 0 to 511
Outputs:
- gram: float32 [2, 4096, 4096], P(None, 'tensor', 'dp')
- scores: float32 [64, 512], P('tensor', 'dp')
The draws below stay inside these ranges and needn't reach their ends.
All inputs are finite; a program needn't handle non-finite values.
Results may differ from the reference program's by a relative error of at most 0.0038.
Values may be sent and summed in bfloat16 or wider, within the bound.
A program may use at most 64 MiB of HBM per device.

```python
import jax
import jax.numpy as jnp
from jax import lax

D = 5120
RANK = 64
SEQ = 128
NQ = 64
EXAMPLES = 512
TOKENS = 65536


def plant(entries, rng, least, high):
    shape = entries.shape
    spot = [jax.random.randint(jax.random.fold_in(rng, axis), (), 0, shape[axis]) for axis in range(len(shape))]
    entries = entries.at[tuple(spot)].set(least)
    longest = shape.index(max(shape))
    spot[longest] = (spot[longest] + 1) % shape[longest]
    return entries.at[tuple(spot)].set(high)


def shard_levels(rng, extent, cuts, smallest, high):
    level, own = 1.0, jax.random.fold_in(rng, 6)
    for position, shards_of in cuts:
        heights = jnp.exp(jax.random.uniform(jax.random.fold_in(own, position), (shards_of,), jnp.float32, smallest / len(cuts), high / len(cuts)))
        level = level * jnp.repeat(heights, extent[position] // shards_of).reshape([-1 if axis == position else 1 for axis in range(len(extent))])
    return level


def scatter_about(stream_key, extent, spread, limit, shards=(), held_as=jnp.bfloat16):
    drawn = spread * jax.random.normal(stream_key, extent, jnp.float32)
    if shards:
        drawn = drawn * shard_levels(stream_key, extent, shards, -0.22, 0.18)
    return jnp.clip(drawn, -limit, limit).astype(held_as)


def setup_inputs(seed: int = 0) -> dict:
    keys = jax.random.split(jax.random.key(seed), 10)
    in_one = scatter_about(keys[0], (TOKENS, D), 1.0, 6.0, ((0, 16), (1, 16)))
    grad_one = scatter_about(keys[1], (TOKENS, D), 1.0, 6.0, ((0, 16), (1, 16)))
    in_two = scatter_about(keys[2], (TOKENS, D), 1.0, 6.0, ((0, 16), (1, 16)))
    grad_two = scatter_about(keys[3], (TOKENS, D), 1.0, 6.0, ((0, 16), (1, 16)))
    proj_in_one = scatter_about(keys[4], (D, RANK), D ** -0.5, 0.078125, ((0, 16),))
    proj_out_one = scatter_about(keys[5], (D, RANK), D ** -0.5, 0.078125, ((0, 16),))
    proj_in_two = scatter_about(keys[6], (D, RANK), D ** -0.5, 0.078125, ((0, 16),))
    proj_out_two = scatter_about(keys[7], (D, RANK), D ** -0.5, 0.078125, ((0, 16),))
    query_index = plant(jax.random.randint(keys[8], (NQ,), 0, EXAMPLES), jax.random.fold_in(keys[8], 1), 0, EXAMPLES - 1).astype(jnp.int32)
    return {"in_one": in_one, "grad_one": grad_one, "in_two": in_two, "grad_two": grad_two, "proj_in_one": proj_in_one, "proj_out_one": proj_out_one, "proj_in_two": proj_in_two, "proj_out_two": proj_out_two, "query_index": query_index}


def layer_features(inputs, grads, proj_in, proj_out):
    xp = jnp.dot(inputs, proj_in, preferred_element_type=jnp.float32).reshape(EXAMPLES, SEQ, RANK)
    gp = jnp.dot(grads, proj_out, preferred_element_type=jnp.float32).reshape(EXAMPLES, SEQ, RANK)
    outer = jnp.einsum('esa,esb->eab', gp, xp, precision=lax.Precision.HIGHEST)
    outer = outer / jnp.sqrt(jnp.float32(SEQ))
    return outer.reshape(EXAMPLES, RANK * RANK).astype(jnp.bfloat16)

def reference(in_one, grad_one, in_two, grad_two, proj_in_one, proj_out_one, proj_in_two, proj_out_two, query_index):
    feat_one = layer_features(in_one, grad_one, proj_in_one, proj_out_one)
    feat_two = layer_features(in_two, grad_two, proj_in_two, proj_out_two)
    grams = []
    for feat in (feat_one, feat_two):
        wide = feat.astype(jnp.float32)
        grams.append(jnp.einsum('ei,ej->ij', wide, wide, precision=lax.Precision.HIGHEST) / EXAMPLES)
    gram = jnp.stack(grams, 0)
    both = jnp.concatenate([feat_one, feat_two], 1)
    query_feat = jnp.take(both, query_index.astype(jnp.int32), axis=0)
    scores = lax.dot_general(query_feat, both, (((1,), (1,)), ((), ())), preferred_element_type=jnp.float32)
    scores = scores / jnp.sqrt(jnp.float32(2 * RANK * RANK))
    return (gram, scores)
```

```python
import jax
import jax.numpy as jnp
from jax import lax
from jax.sharding import PartitionSpec as P

SEQ = 128


def local(
    in_one,
    grad_one,
    in_two,
    grad_two,
    proj_in_one,
    proj_out_one,
    proj_in_two,
    proj_out_two,
    query_index,
):
    tok_rows = in_one.shape[0]
    rank = proj_in_one.shape[1]
    examples_dev = tok_rows // SEQ
    tensor_count = lax.axis_size("tensor")
    share = rank * rank // tensor_count
    scale_seq = jnp.sqrt(jnp.float32(SEQ))
    partial_proj = jnp.concatenate(
        [
            jnp.dot(in_one, proj_in_one, preferred_element_type=jnp.float32),
            jnp.dot(grad_one, proj_out_one, preferred_element_type=jnp.float32),
            jnp.dot(in_two, proj_in_two, preferred_element_type=jnp.float32),
            jnp.dot(grad_two, proj_out_two, preferred_element_type=jnp.float32),
        ],
        1,
    )
    summed = lax.psum_scatter(partial_proj, "tensor", scatter_dimension=0, tiled=True)
    mine = examples_dev // tensor_count
    summed = summed.reshape(mine, SEQ, 2, 2, rank)
    outer = jnp.einsum(
        "esla,eslb->elab", summed[:, :, :, 1], summed[:, :, :, 0], precision=lax.Precision.HIGHEST
    )
    feat = (outer / scale_seq).reshape(mine, 2, rank * rank).astype(jnp.bfloat16)
    dp_count = lax.axis_size("dp")
    examples_all = examples_dev * dp_count
    by_tensor = feat.reshape(mine, 2, tensor_count, share)
    own_feat = lax.all_to_all(by_tensor, "tensor", 2, 0, tiled=True).reshape(examples_dev, 2, share)
    rows = lax.all_gather(own_feat, "dp", axis=0, tiled=True)
    share_dp = rank * rank // dp_count
    by_dp = feat.reshape(mine, 2, dp_count, share_dp)
    cols = lax.all_to_all(by_dp, "dp", 2, 0, tiled=True).reshape(dp_count, 1, mine, 2, share_dp)
    cols = lax.all_gather(cols, "tensor", axis=1, tiled=True).reshape(examples_all, 2, share_dp)
    gram = jnp.einsum("eli,elj->lij", rows, cols, preferred_element_type=jnp.float32) / examples_all
    flat = rows.reshape(examples_all, 2 * share)
    selector = (query_index[:, None] == jnp.arange(examples_all, dtype=jnp.int32)[None, :]).astype(
        jnp.bfloat16
    )
    query_feat = jnp.dot(selector, flat, preferred_element_type=jnp.float32).astype(jnp.bfloat16)
    own_flat = own_feat.reshape(examples_dev, 2 * share)
    score_part = lax.dot_general(
        query_feat, own_flat, (((1,), (1,)), ((), ())), preferred_element_type=jnp.float32
    )
    scores = lax.psum_scatter(score_part, "tensor", scatter_dimension=0, tiled=True)
    scores = scores / jnp.sqrt(jnp.float32(2 * rank * rank))
    return (gram, scores)


def solution(mesh):
    in_specs = (
        P("dp", "tensor"),
        P("dp", "tensor"),
        P("dp", "tensor"),
        P("dp", "tensor"),
        P("tensor", None),
        P("tensor", None),
        P("tensor", None),
        P("tensor", None),
        P(),
    )
    out_specs = (P(None, "tensor", "dp"), P("tensor", "dp"))
    return jax.shard_map(local, mesh=mesh, in_specs=in_specs, out_specs=out_specs, check_vma=False)
```

```python
import math

import jax
import jax.numpy as jnp
from jax import lax
from jax.experimental import pallas as pl
from jax.experimental.pallas import tpu as pltpu
from jax.sharding import PartitionSpec as P

SEQ = 128
RANK = 64
GROUP = 16
RING = 8
LANES = 128
PACK = 2 * SEQ + 16
MESH = pl.DeviceIdType.MESH
AWAY = (4, -3, 3, -2, 2, -1, 1, 0)


def encode(dst, layers):
    keys = []
    for which, values in enumerate(layers):
        top = jnp.max(jnp.abs(values), axis=0, keepdims=True)
        key = jnp.ceil(8.0 * jnp.log2(jnp.maximum(top, 1e-30)) + 0.1)
        scaled = jnp.round(values * jnp.exp2(15.0 - key * 0.125))
        dst[which * SEQ : (which + 1) * SEQ, :] = scaled.astype(jnp.int32).astype(jnp.int16)
        keys.append(key)
    row = lax.broadcasted_iota(jnp.int32, (16, LANES), 0)
    both = jnp.where(row < 8, keys[0], keys[1])
    dst[2 * SEQ : PACK, :] = both.astype(jnp.int32).astype(jnp.int16)


def decode(src):
    keys = src[2 * SEQ : PACK, :].astype(jnp.int32).astype(jnp.float32)
    out = []
    for which in range(2):
        step = jnp.exp2(keys[8 * which : 8 * which + 1, :] * 0.125 - 15.0)
        whole = src[which * SEQ : (which + 1) * SEQ, :].astype(jnp.int32).astype(jnp.float32)
        out.append(whole * step)
    return out


def add(one, two):
    return [a + b for a, b in zip(one, two)]


def kernel(
    in_one, grad_one, in_two, grad_two, w_in_one, w_out_one, w_in_two, w_out_two, query,
    gram, scores,
    tok, wide, part, a_out, a_got, b_out, b_got, x_out, x_got, square, slices, land_t, land_d,
    rows, cols, swap, pick, turned, score_out, score_got,
    in_sem, a_ss, a_rs, b_ss, b_rs, x_ss, x_rs, lt_ss, lt_rs, ld_ss, ld_rs,
    t_ss, t_rs, d_ss, d_rs, dx_ss, dx_rs, s_ss, s_rs,
):
    d = lax.axis_index("dp")
    t = lax.axis_index("tensor")
    z, xh = t // 2, t % 2
    way = 1 - 2 * (d % 2)
    owners = [lax.rem(z + way * step + RING, RING) for step in AWAY]
    forward = (d, lax.rem(z + way + RING, RING) * 2 + xh)
    backward = (d, lax.rem(z - way + RING, RING) * 2 + xh)
    partner = (d, z * 2 + 1 - xh)
    sends = []

    def send(src, dst, ss, rs, device):
        copy = pltpu.make_async_remote_copy(
            src_ref=src, dst_ref=dst, send_sem=ss, recv_sem=rs, device_id=device, device_id_type=MESH
        )
        copy.start()
        sends.append(copy)

    def landed(ref, rs):
        pltpu.make_async_copy(ref, ref, rs).wait()

    loads = {}
    for i in range(RING):
        for half in range(2):
            start = pl.multiple_of((half * GROUP + 2 * owners[i]) * SEQ, 2 * SEQ)
            for k, source in enumerate((in_one, grad_one, in_two, grad_two)):
                copy = pltpu.make_async_copy(
                    source.at[pl.ds(start, 2 * SEQ)],
                    tok.at[k, pl.ds(start, 2 * SEQ)],
                    in_sem.at[i, half, k],
                )
                copy.start()
                loads[i, half, k] = copy

    barrier = pltpu.get_barrier_semaphore()
    for k in range(1, GROUP):
        pl.semaphore_signal(
            barrier, inc=1, device_id=(d, lax.rem(t + k, GROUP)), device_id_type=MESH
        )
        pl.semaphore_signal(
            barrier, inc=1, device_id=(lax.rem(d + k, GROUP), t), device_id_type=MESH
        )

    blank = jnp.zeros((w_in_one.shape[0], RANK), jnp.bfloat16)
    for k, weight in enumerate((w_in_one, w_out_one, w_in_two, w_out_two)):
        sides = [weight[...], blank] if k % 2 == 0 else [blank, weight[...]]
        wide[k] = jnp.concatenate(sides, 1)

    def project(i, half):
        first = half * GROUP + 2 * owners[i]
        start = pl.multiple_of(first * SEQ, 2 * SEQ)
        for k in range(4):
            loads[i, half, k].wait()
        for layer in range(2):
            both = jnp.dot(
                tok[2 * layer, pl.ds(start, 2 * SEQ), :],
                wide[2 * layer],
                preferred_element_type=jnp.float32,
            ) + jnp.dot(
                tok[2 * layer + 1, pl.ds(start, 2 * SEQ), :],
                wide[2 * layer + 1],
                preferred_element_type=jnp.float32,
            )
            part[first, layer] = both[:SEQ]
            part[first + 1, layer] = both[SEQ:]

    def own(half, owner, side):
        index = half * GROUP + 2 * owner + side
        return [part[index, 0], part[index, 1]]

    def ring_a(i):
        for side in range(2):
            total = own(0, owners[i], side)
            if i >= 2:
                landed(a_got.at[i - 2, side], a_rs.at[i - 2, side])
                total = add(total, decode(a_got.at[i - 2, side]))
            encode(a_out.at[i, side], total)
            send(
                a_out.at[i, side], a_got.at[i, side], a_ss.at[i, side], a_rs.at[i, side],
                forward if i % 2 == 0 else backward,
            )

    def pair(i):
        encode(x_out.at[i], own(1, owners[i], 1 - xh))
        send(x_out.at[i], x_got.at[i], x_ss.at[i], x_rs.at[i], partner)

    def ring_b(i):
        landed(x_got.at[i], x_rs.at[i])
        total = add(own(1, owners[i], xh), decode(x_got.at[i]))
        if i >= 2:
            landed(b_got.at[i - 2], b_rs.at[i - 2])
            total = add(total, decode(b_got.at[i - 2]))
        encode(b_out.at[i], total)
        send(
            b_out.at[i], b_got.at[i], b_ss.at[i], b_rs.at[i], forward if i % 2 == 0 else backward
        )

    for i in range(RING + 1):
        if i < RING:
            project(i, 0)
            if i == 0:
                pl.semaphore_wait(barrier, 2 * (GROUP - 1))
            if i < RING - 1:
                ring_a(i)
            project(i, 1)
            pair(i)
        if i >= 2:
            ring_b(i - 2)

    for side in range(2):
        for i in (5, 6):
            landed(a_got.at[i, side], a_rs.at[i, side])

    def over_z(side):
        total = own(0, z, side)
        for i in (5, 6):
            total = add(total, decode(a_got.at[i, side]))
        return total

    encode(x_out.at[RING], over_z(1 - xh))
    send(x_out.at[RING], x_got.at[RING], x_ss.at[RING], x_rs.at[RING], partner)

    at_row = lax.broadcasted_iota(jnp.int32, (GROUP * 32, GROUP * 32), 0)
    at_col = lax.broadcasted_iota(jnp.int32, (GROUP * 32, GROUP * 32), 1)
    mirrored = (at_row % 16) * 32 + (at_row // 16 % 2) * 16 + at_row // 32
    swap[...] = jnp.where(at_col == mirrored, 1.0, 0.0).astype(jnp.bfloat16)
    example = lax.broadcasted_iota(jnp.int32, pick.shape, 0)
    pick[...] = jnp.where(example == query[...], 1.0, 0.0).astype(jnp.bfloat16)
    score_out[...] = jnp.zeros_like(score_out)

    def features(half, sums):
        for layer in range(2):
            outer = lax.dot_general(
                sums[layer], sums[layer], (((0,), (0,)), ((), ())),
                precision=lax.Precision.HIGHEST, preferred_element_type=jnp.float32,
            )
            scaled = outer[RANK:, :] / jnp.float32(math.sqrt(SEQ))
            square[...] = scaled.astype(jnp.bfloat16).astype(jnp.float32)
            for pair_of in range(2):
                even = square[pl.ds(2 * pair_of, GROUP, stride=4), :]
                odd = square[pl.ds(2 * pair_of + 1, GROUP, stride=4), :]
                slices[pl.ds(half * 4 + layer * 2 + pair_of, GROUP, stride=8), :] = jnp.concatenate(
                    [even[:, :RANK], odd[:, :RANK]], 1
                )

    for i in (5, 6):
        landed(b_got.at[i], b_rs.at[i])
    landed(x_got.at[RING - 1], x_rs.at[RING - 1])
    total = add(own(1, z, xh), decode(x_got.at[RING - 1]))
    for i in (5, 6):
        total = add(total, decode(b_got.at[i]))
    features(1, total)
    landed(x_got.at[RING], x_rs.at[RING])
    features(0, add(over_z(xh), decode(x_got.at[RING])))

    def tile(index):
        return pl.ds(pl.multiple_of(8 * index, 8), 8)

    for k in range(1, GROUP):
        to = lax.rem(t + k, GROUP)
        send(slices.at[tile(to)], land_t.at[tile(t)], lt_ss.at[k], lt_rs.at[k], (d, to))
        to = lax.rem(d + k, GROUP)
        send(slices.at[tile(to)], land_d.at[tile(d)], ld_ss.at[k], ld_rs.at[k], (to, t))
    land_t[tile(t), :] = slices[tile(t), :]
    land_d[tile(d), :] = slices[tile(d), :]

    def gather(land, block, rs):
        for k in range(1, GROUP):
            landed(land.at[pl.ds(0, 8)], rs.at[k])
        for half in range(2):
            lanes = [land[pl.ds(half * 4 + k, GROUP, stride=8), :] for k in range(4)]
            block[half * GROUP : (half + 1) * GROUP, :] = jnp.concatenate(lanes, 1).astype(
                jnp.bfloat16
            )

    def pass_on(step, stream, go):
        side = xh if stream == 0 else 1 - xh
        sign = -way if go == 0 else way
        block = lax.rem(z + sign * step + RING, RING) * 2 + side
        i = 2 * step + go
        send(
            cols.at[block], cols.at[block], d_ss.at[i, stream], d_rs.at[i, stream],
            forward if go == 0 else backward,
        )

    gather(land_d, cols.at[t], ld_rs)
    send(cols.at[t], cols.at[t], dx_ss.at[0], dx_rs.at[0], partner)
    pass_on(0, 0, 0)
    pass_on(0, 0, 1)
    gather(land_t, rows.at[d], lt_rs)
    for k in range(1, GROUP):
        send(rows.at[d], rows.at[d], t_ss.at[k], t_rs.at[k], (lax.rem(d + k, GROUP), t))
    for step in range(4):
        for stream in range(2):
            if step == 0 and stream == 0:
                continue
            for go in range(2):
                if step == 3 and go == 1:
                    continue
                if step == 0:
                    if go == 0:
                        landed(cols.at[0], dx_rs.at[0])
                else:
                    landed(cols.at[0], d_rs.at[2 * (step - 1) + go, stream])
                pass_on(step, stream, go)

    for k in range(1, GROUP):
        landed(rows.at[0], t_rs.at[k])
    mine = rows[d]
    all_rows = rows[...].reshape(GROUP * 32, 4 * LANES)
    query_feat = lax.dot_general(
        pick[...], all_rows, (((0,), (0,)), ((), ())), preferred_element_type=jnp.float32
    ).astype(jnp.bfloat16)
    partial_scores = lax.dot_general(
        query_feat, mine, (((1,), (1,)), ((), ())), preferred_element_type=jnp.float32
    )
    for k in range(GROUP):
        score_out[8 * k : 8 * k + 4, 0:32] = partial_scores[4 * k : 4 * k + 4, :]
    for k in range(1, GROUP):
        to = lax.rem(t + k, GROUP)
        send(score_out.at[tile(to)], score_got.at[tile(t)], s_ss.at[k], s_rs.at[k], (d, to))
    score_got[tile(t), :] = score_out[tile(t), :]
    turned[...] = lax.dot_general(
        all_rows, swap[...], (((0,), (0,)), ((), ())), preferred_element_type=jnp.float32
    ).astype(jnp.bfloat16)

    for stream in range(2):
        for i in (4, 5, 6):
            if i != 4:
                landed(cols.at[0], d_rs.at[i, stream])
    all_cols = cols[...].reshape(GROUP * 32, 4 * LANES)
    for layer in range(2):
        span = slice(layer * 2 * LANES, (layer + 1) * 2 * LANES)
        gram[layer] = jnp.dot(
            turned[span, :], all_cols[:, span], preferred_element_type=jnp.float32
        ) * jnp.float32(1.0 / 512)

    for k in range(1, GROUP):
        landed(score_got.at[pl.ds(0, 8)], s_rs.at[k])
    total = score_got[0:8, :]
    for k in range(1, GROUP):
        total = total + score_got[8 * k : 8 * k + 8, :]
    scores[...] = total[0:4, 0:32] / jnp.float32(math.sqrt(2 * RANK * RANK))
    for copy in sends:
        copy.wait_send()


def local(*args):
    tokens, width = args[0].shape
    query = args[-1].reshape(1, -1)
    dma = pltpu.SemaphoreType.DMA
    f32, bf16, i16 = jnp.float32, jnp.bfloat16, jnp.int16
    vmem = pltpu.VMEM
    scratch = [
        vmem((4, tokens, width), bf16),
        vmem((4, width, LANES), bf16),
        vmem((tokens // SEQ, 2, SEQ, LANES), f32),
        vmem((7, 2, PACK, LANES), i16),
        vmem((7, 2, PACK, LANES), i16),
        vmem((7, PACK, LANES), i16),
        vmem((7, PACK, LANES), i16),
        vmem((RING + 1, PACK, LANES), i16),
        vmem((RING + 1, PACK, LANES), i16),
        vmem((RANK, LANES), f32),
        vmem((8 * GROUP, LANES), f32),
        vmem((8 * GROUP, LANES), f32),
        vmem((8 * GROUP, LANES), f32),
        vmem((GROUP, 32, 4 * LANES), bf16),
        vmem((GROUP, 32, 4 * LANES), bf16),
        vmem((GROUP * 32, GROUP * 32), bf16),
        vmem((GROUP * 32, query.shape[1]), bf16),
        vmem((4 * LANES, GROUP * 32), bf16),
        vmem((8 * GROUP, LANES), f32),
        vmem((8 * GROUP, LANES), f32),
        dma((RING, 2, 4)),
        dma((7, 2)), dma((7, 2)),
        dma((7,)), dma((7,)),
        dma((RING + 1,)), dma((RING + 1,)),
        dma((GROUP,)), dma((GROUP,)),
        dma((GROUP,)), dma((GROUP,)),
        dma((GROUP,)), dma((GROUP,)),
        dma((7, 2)), dma((7, 2)),
        dma((1,)), dma((1,)),
        dma((GROUP,)), dma((GROUP,)),
    ]
    anywhere = pl.BlockSpec(memory_space=pl.ANY)
    in_vmem = pl.BlockSpec(memory_space=pltpu.VMEM)
    return pl.pallas_call(
        kernel,
        out_shape=(
            jax.ShapeDtypeStruct((2, 256, 256), f32),
            jax.ShapeDtypeStruct((4, 32), f32),
        ),
        in_specs=[anywhere] * 4 + [in_vmem] * 5,
        out_specs=(in_vmem, in_vmem),
        scratch_shapes=scratch,
        compiler_params=pltpu.CompilerParams(
            collective_id=0, has_side_effects=True, vmem_limit_bytes=48 << 20
        ),
    )(*args[:-1], query)


def solution(mesh):
    in_specs = (
        P("dp", "tensor"),
        P("dp", "tensor"),
        P("dp", "tensor"),
        P("dp", "tensor"),
        P("tensor", None),
        P("tensor", None),
        P("tensor", None),
        P("tensor", None),
        P(),
    )
    out_specs = (P(None, "tensor", "dp"), P("tensor", "dp"))
    return jax.shard_map(local, mesh=mesh, in_specs=in_specs, out_specs=out_specs, check_vma=False)
```

```python
import math

import jax
import jax.numpy as jnp
from jax import lax
from jax.experimental import pallas as pl
from jax.experimental.pallas import tpu as pltpu
from jax.sharding import PartitionSpec as P

SEQ = 128
RANK = 64
GROUP = 16
RING = 8
LANES = 128
PACK = 4 * RANK + 16
MESH = pl.DeviceIdType.MESH
AWAY = (4, -3, 3, -2, 2, -1, 1, 0)


def encode(dst, layers):
    keys = []
    for which, values in enumerate(layers):
        for side in range(2):
            some = values[side * RANK : (side + 1) * RANK]
            top = jnp.max(jnp.abs(some), axis=0, keepdims=True)
            key = jnp.ceil(8.0 * jnp.log2(jnp.maximum(top, 1e-30)) + 0.1)
            scaled = jnp.round(some * jnp.exp2(15.0 - key * 0.125))
            start = (2 * which + side) * RANK
            dst[start : start + RANK, :] = scaled.astype(jnp.int32).astype(jnp.int16)
            keys.append(key)
    row = lax.broadcasted_iota(jnp.int32, (16, SEQ), 0)
    both = jnp.where(row < 4, keys[0], keys[1])
    both = jnp.where(row < 8, both, jnp.where(row < 12, keys[2], keys[3]))
    dst[4 * RANK : PACK, :] = both.astype(jnp.int32).astype(jnp.int16)


def decode(src):
    keys = src[4 * RANK : PACK, :].astype(jnp.int32).astype(jnp.float32)
    out = []
    for which in range(4):
        step = jnp.exp2(keys[4 * which : 4 * which + 1, :] * 0.125 - 15.0)
        whole = src[which * RANK : (which + 1) * RANK, :].astype(jnp.int32).astype(jnp.float32)
        out.append(whole * step)
    return [jnp.concatenate(out[:2], 0), jnp.concatenate(out[2:], 0)]


def add(one, two):
    return [a + b for a, b in zip(one, two)]


def kernel(
    in_one, grad_one, in_two, grad_two, w_in_one, w_out_one, w_in_two, w_out_two, asked,
    gram, scores,
    tok, weights, query, part, a_out, a_got, b_out, b_got, x_out, x_got, square, slices, land_t, land_d,
    rows, cols, swap, pick, turned, score_out, score_got,
    in_sem, w_sem, q_sem, a_ss, a_rs, b_ss, b_rs, x_ss, x_rs, lt_ss, lt_rs, ld_ss, ld_rs,
    t_ss, t_rs, d_ss, d_rs, s_ss, s_rs,
):
    d = lax.axis_index("dp")
    t = lax.axis_index("tensor")
    z, xh = t // 2, t % 2
    way = 1 - 2 * (d % 2)
    owners = [lax.rem(z + way * step + RING, RING) for step in AWAY]
    forward = (d, lax.rem(z + way + RING, RING) * 2 + xh)
    backward = (d, lax.rem(z - way + RING, RING) * 2 + xh)
    partner = (d, z * 2 + 1 - xh)
    def send(src, dst, ss, rs, device):
        pltpu.make_async_remote_copy(
            src_ref=src, dst_ref=dst, send_sem=ss, recv_sem=rs, device_id=device, device_id_type=MESH
        ).start()

    def landed(ref, sem):
        pltpu.make_async_copy(ref, ref, sem).wait()

    barrier = pltpu.get_barrier_semaphore()
    for k in range(1, GROUP):
        pl.semaphore_signal(
            barrier, inc=1, device_id=(d, lax.rem(t + k, GROUP)), device_id_type=MESH
        )
        pl.semaphore_signal(
            barrier, inc=1, device_id=(lax.rem(d + k, GROUP), t), device_id_type=MESH
        )

    def load(i):
        for half in range(2):
            start = pl.multiple_of((half * GROUP + 2 * owners[i]) * SEQ, 2 * SEQ)
            for k, source in enumerate((in_one, grad_one, in_two, grad_two)):
                pltpu.make_async_copy(
                    source.at[:, pl.ds(start, 2 * SEQ)],
                    tok.at[k, :, pl.ds(start, 2 * SEQ)],
                    in_sem.at[i, half],
                ).start()

    for k, weight in enumerate((w_in_one, w_out_one, w_in_two, w_out_two)):
        pltpu.make_async_copy(weight, weights.at[k], w_sem.at[0]).start()
    for i in range(3):
        load(i)
    pltpu.make_async_copy(asked, query, q_sem.at[0]).start()
    landed(weights, w_sem.at[0])

    def project(i, half):
        first = half * GROUP + 2 * owners[i]
        start = pl.multiple_of(first * SEQ, 2 * SEQ)
        landed(tok.at[:, :, pl.ds(start, 2 * SEQ)], in_sem.at[i, half])
        for k in range(4):
            both = jnp.dot(
                weights[k],
                tok[k, :, pl.ds(start, 2 * SEQ)],
                preferred_element_type=jnp.float32,
            )
            span = slice(k % 2 * RANK, (k % 2 + 1) * RANK)
            part[first, k // 2, span, :] = both[:, :SEQ]
            part[first + 1, k // 2, span, :] = both[:, SEQ:]

    def own(half, owner, side):
        index = half * GROUP + 2 * owner + side
        return [part[index, 0], part[index, 1]]

    def ring_a(i):
        for side in range(2):
            total = own(0, owners[i], side)
            if i >= 2:
                landed(a_got.at[i - 2, side], a_rs.at[i - 2, side])
                total = add(total, decode(a_got.at[i - 2, side]))
            encode(a_out.at[i, side], total)
            send(
                a_out.at[i, side], a_got.at[i, side], a_ss.at[0], a_rs.at[i, side],
                forward if i % 2 == 0 else backward,
            )

    def pair(i):
        encode(x_out.at[i], own(1, owners[i], 1 - xh))
        send(x_out.at[i], x_got.at[i], x_ss.at[0], x_rs.at[i], partner)

    def ring_b(i):
        landed(x_got.at[i], x_rs.at[i])
        total = add(own(1, owners[i], xh), decode(x_got.at[i]))
        if i >= 2:
            landed(b_got.at[i - 2], b_rs.at[i - 2])
            total = add(total, decode(b_got.at[i - 2]))
        encode(b_out.at[i], total)
        send(
            b_out.at[i], b_got.at[i], b_ss.at[0], b_rs.at[i], forward if i % 2 == 0 else backward
        )

    for i in range(RING + 1):
        if i < RING:
            project(i, 0)
            if i + 3 < RING:
                load(i + 3)
            if i == 0:
                pl.semaphore_wait(barrier, 2 * (GROUP - 1))
            if i < RING - 1:
                ring_a(i)
            project(i, 1)
            pair(i)
        if i >= 2:
            ring_b(i - 2)

    for side in range(2):
        for i in (5, 6):
            landed(a_got.at[i, side], a_rs.at[i, side])

    def over_z(side):
        total = own(0, z, side)
        for i in (5, 6):
            total = add(total, decode(a_got.at[i, side]))
        return total

    encode(x_out.at[RING], over_z(1 - xh))
    send(x_out.at[RING], x_got.at[RING], x_ss.at[0], x_rs.at[RING], partner)

    at_row = lax.broadcasted_iota(jnp.int32, (GROUP * 32, GROUP * 32), 0)
    at_col = lax.broadcasted_iota(jnp.int32, (GROUP * 32, GROUP * 32), 1)
    mirrored = (at_row % 16) * 32 + (at_row // 16 % 2) * 16 + at_row // 32
    swap[...] = jnp.where(at_col == mirrored, 1.0, 0.0).astype(jnp.bfloat16)
    landed(query, q_sem.at[0])
    row = lax.broadcasted_iota(jnp.int32, pick.shape, 0)
    example = (row // 32 % 8 * 2 + row // 256) * 32 + row % 32
    pick[...] = jnp.where(example == query[...], 1.0, 0.0).astype(jnp.bfloat16)
    score_out[...] = jnp.zeros_like(score_out)

    def features(half, sums):
        for layer in range(2):
            outer = lax.dot_general(
                sums[layer], sums[layer], (((1,), (1,)), ((), ())),
                precision=lax.Precision.HIGHEST, preferred_element_type=jnp.float32,
            )
            scaled = outer[RANK:, :] / jnp.float32(math.sqrt(SEQ))
            square[...] = scaled.astype(jnp.bfloat16).astype(jnp.float32)
            for pair_of in range(2):
                even = square[pl.ds(2 * pair_of, GROUP, stride=4), :]
                odd = square[pl.ds(2 * pair_of + 1, GROUP, stride=4), :]
                slices[pl.ds(half * 4 + layer * 2 + pair_of, GROUP, stride=8), :] = jnp.concatenate(
                    [even[:, :RANK], odd[:, :RANK]], 1
                )

    for i in (5, 6):
        landed(b_got.at[i], b_rs.at[i])
    landed(x_got.at[RING - 1], x_rs.at[RING - 1])
    total = add(own(1, z, xh), decode(x_got.at[RING - 1]))
    for i in (5, 6):
        total = add(total, decode(b_got.at[i]))
    features(1, total)
    landed(x_got.at[RING], x_rs.at[RING])
    features(0, add(over_z(xh), decode(x_got.at[RING])))

    place = d % 2 * 8 + d // 2

    def along(steps):
        return lax.rem(z + steps + RING, RING)

    def tile(index):
        return pl.ds(pl.multiple_of(8 * index, 8), 8)

    for k in range(1, GROUP):
        to = lax.rem(t + k, GROUP)
        send(slices.at[tile(to)], land_t.at[tile(t)], lt_ss.at[0], lt_rs.at[0], (d, to))
    for k in range(1, GROUP):
        to = lax.rem(d + k, GROUP)
        send(slices.at[tile(to)], land_d.at[tile(place)], ld_ss.at[0], ld_rs.at[0], (to, t))
    land_t[tile(t), :] = slices[tile(t), :]
    land_d[tile(place), :] = slices[tile(d), :]

    def gather(land, block, rs):
        landed(land.at[pl.ds(0, 8 * (GROUP - 1))], rs.at[0])
        for half in range(2):
            lanes = [land[pl.ds(half * 4 + k, GROUP, stride=8), :] for k in range(4)]
            block[half * GROUP : (half + 1) * GROUP, :] = jnp.concatenate(lanes, 1).astype(
                jnp.bfloat16
            )

    gather(land_t, rows.at[place], lt_rs)
    for k in range(1, 8):
        send(rows.at[place], rows.at[place], t_ss.at[0], t_rs.at[0], (lax.rem(d + 2 * k, GROUP), t))

    gather(land_d, cols.at[t], ld_rs)
    for i, steps in enumerate((2, -2, 1, -1, 0)):
        for flip in range(2):
            if steps or flip:
                to = along(steps) * 2 + (1 - xh if flip else xh)
                send(cols.at[t], cols.at[t], d_ss.at[0], d_rs.at[0 if i < 2 else 1], (d, to))

    landed(rows.at[pl.ds(0, 7)], t_rs.at[0])
    block = pl.ds(d % 2 * 8, 8)
    sibling = (d + 1 - 2 * (d % 2), t)
    send(rows.at[block], rows.at[block], t_ss.at[1], t_rs.at[1], sibling)

    landed(cols.at[pl.ds(0, 4)], d_rs.at[0])
    for held, steps in ((-2 * way, way), (-2 * way, 2 * way), (2 * way, -way)):
        block = pl.ds(2 * along(held), 2)
        to = along(steps) * 2 + xh
        send(cols.at[block], cols.at[block], d_ss.at[1], d_rs.at[2], (d, to))

    landed(rows.at[pl.ds(0, 8)], t_rs.at[1])
    mine = rows[place]
    all_rows = rows[...].reshape(GROUP * 32, 4 * LANES)
    query_feat = lax.dot_general(
        pick[...], all_rows, (((0,), (0,)), ((), ())), preferred_element_type=jnp.float32
    ).astype(jnp.bfloat16)
    partial_scores = lax.dot_general(
        query_feat, mine, (((1,), (1,)), ((), ())), preferred_element_type=jnp.float32
    )
    for k in range(GROUP):
        score_out[8 * k : 8 * k + 4, 0:32] = partial_scores[4 * k : 4 * k + 4, :]
    for k in range(1, GROUP):
        to = lax.rem(t + k, GROUP)
        send(score_out.at[tile(to)], score_got.at[tile(t)], s_ss.at[0], s_rs.at[0], (d, to))
    score_got[tile(t), :] = score_out[tile(t), :]
    turned[...] = lax.dot_general(
        all_rows, swap[...], (((0,), (0,)), ((), ())), preferred_element_type=jnp.float32
    ).astype(jnp.bfloat16)

    landed(cols.at[pl.ds(0, 5)], d_rs.at[1])
    landed(cols.at[pl.ds(0, 6)], d_rs.at[2])
    all_cols = cols[...].reshape(GROUP * 32, 4 * LANES)
    for layer in range(2):
        span = slice(layer * 2 * LANES, (layer + 1) * 2 * LANES)
        gram[layer] = jnp.dot(
            turned[span, :], all_cols[:, span], preferred_element_type=jnp.float32
        ) * jnp.float32(1.0 / 512)

    landed(score_got.at[pl.ds(0, 8 * (GROUP - 1))], s_rs.at[0])
    total = score_got[0:8, :]
    for k in range(1, GROUP):
        total = total + score_got[8 * k : 8 * k + 8, :]
    scores[...] = total[0:4, 0:32] / jnp.float32(math.sqrt(2 * RANK * RANK))

    tiles = pl.ds(0, 8 * (GROUP - 1))
    for ref, sem in (
        (a_out, a_ss.at[0]),
        (b_out, b_ss.at[0]),
        (x_out, x_ss.at[0]),
        (land_t.at[tiles], lt_ss.at[0]),
        (land_d.at[tiles], ld_ss.at[0]),
        (rows.at[pl.ds(0, 7)], t_ss.at[0]),
        (rows.at[pl.ds(0, 8)], t_ss.at[1]),
        (cols.at[pl.ds(0, 9)], d_ss.at[0]),
        (cols.at[pl.ds(0, 6)], d_ss.at[1]),
        (score_got.at[tiles], s_ss.at[0]),
    ):
        landed(ref, sem)


def local(*args):
    tokens, width = args[0].shape
    query = args[-1].reshape(1, -1)
    dma = pltpu.SemaphoreType.DMA
    f32, bf16, i16 = jnp.float32, jnp.bfloat16, jnp.int16
    vmem = pltpu.VMEM
    scratch = [
        vmem((4, width, tokens), bf16),
        vmem((4, RANK, width), bf16),
        vmem(query.shape, jnp.int32),
        vmem((tokens // SEQ, 2, LANES, SEQ), f32),
        vmem((7, 2, PACK, LANES), i16),
        vmem((7, 2, PACK, LANES), i16),
        vmem((7, PACK, LANES), i16),
        vmem((7, PACK, LANES), i16),
        vmem((RING + 1, PACK, LANES), i16),
        vmem((RING + 1, PACK, LANES), i16),
        vmem((RANK, LANES), f32),
        vmem((8 * GROUP, LANES), f32),
        vmem((8 * GROUP, LANES), f32),
        vmem((8 * GROUP, LANES), f32),
        vmem((GROUP, 32, 4 * LANES), bf16),
        vmem((GROUP, 32, 4 * LANES), bf16),
        vmem((GROUP * 32, GROUP * 32), bf16),
        vmem((GROUP * 32, query.shape[1]), bf16),
        vmem((4 * LANES, GROUP * 32), bf16),
        vmem((8 * GROUP, LANES), f32),
        vmem((8 * GROUP, LANES), f32),
        dma((RING, 2)), dma((1,)), dma((1,)),
        dma((1,)), dma((7, 2)),
        dma((1,)), dma((7,)),
        dma((1,)), dma((RING + 1,)),
        dma((1,)), dma((1,)),
        dma((1,)), dma((1,)),
        dma((2,)), dma((2,)),
        dma((2,)), dma((3,)),
        dma((1,)), dma((1,)),
    ]
    in_hbm = pl.BlockSpec(memory_space=pltpu.HBM)
    in_vmem = pl.BlockSpec(memory_space=pltpu.VMEM)
    return pl.pallas_call(
        kernel,
        out_shape=(
            jax.ShapeDtypeStruct((2, 256, 256), f32),
            jax.ShapeDtypeStruct((4, 32), f32),
        ),
        in_specs=[in_hbm] * 9,
        out_specs=(in_vmem, in_vmem),
        scratch_shapes=scratch,
        compiler_params=pltpu.CompilerParams(
            collective_id=0, has_side_effects=True, vmem_limit_bytes=58 << 20
        ),
    )(*[arg.T for arg in args[:-1]], query)


def solution(mesh):
    in_specs = (
        P("dp", "tensor"),
        P("dp", "tensor"),
        P("dp", "tensor"),
        P("dp", "tensor"),
        P("tensor", None),
        P("tensor", None),
        P("tensor", None),
        P("tensor", None),
        P(),
    )
    out_specs = (P(None, "tensor", "dp"), P("tensor", "dp"))
    return jax.shard_map(local, mesh=mesh, in_specs=in_specs, out_specs=out_specs, check_vma=False)
```

```python
import math

import jax
import jax.numpy as jnp
from jax import lax
from jax.experimental import pallas as pl
from jax.experimental.pallas import tpu as pltpu
from jax.sharding import PartitionSpec as P

SEQ = 128
RANK = 64
GROUP = 16
RING = 8
LANES = 128
PACK = 4 * RANK + 16
MESH = pl.DeviceIdType.MESH
AWAY = (4, -3, 3, -2, 2, -1, 1, 0)


def encode(dst, layers):
    keys = []
    for which, values in enumerate(layers):
        for side in range(2):
            some = values[side * RANK : (side + 1) * RANK]
            top = jnp.max(jnp.abs(some), axis=0, keepdims=True)
            key = jnp.ceil(8.0 * jnp.log2(jnp.maximum(top, 1e-30)) + 0.1)
            scaled = jnp.round(some * jnp.exp2(15.0 - key * 0.125))
            start = (2 * which + side) * RANK
            dst[start : start + RANK, :] = scaled.astype(jnp.int32).astype(jnp.int16)
            keys.append(key)
    row = lax.broadcasted_iota(jnp.int32, (16, SEQ), 0)
    both = jnp.where(row < 4, keys[0], keys[1])
    both = jnp.where(row < 8, both, jnp.where(row < 12, keys[2], keys[3]))
    dst[4 * RANK : PACK, :] = both.astype(jnp.int32).astype(jnp.int16)


def decode(src):
    keys = src[4 * RANK : PACK, :].astype(jnp.int32).astype(jnp.float32)
    out = []
    for which in range(4):
        step = jnp.exp2(keys[4 * which : 4 * which + 1, :] * 0.125 - 15.0)
        whole = src[which * RANK : (which + 1) * RANK, :].astype(jnp.int32).astype(jnp.float32)
        out.append(whole * step)
    return [jnp.concatenate(out[:2], 0), jnp.concatenate(out[2:], 0)]


def add(one, two):
    return [a + b for a, b in zip(one, two)]


def kernel(
    in_one, grad_one, in_two, grad_two, w_in_one, w_out_one, w_in_two, w_out_two, asked,
    gram, scores,
    tok, weights, query, part, a_out, a_got, b_out, b_got, x_out, x_got, square, slices, land_t, land_d,
    rows, cols, swap, pick, turned, score_out, score_got,
    in_sem, w_sem, q_sem, a_ss, a_rs, b_ss, b_rs, x_ss, x_rs, lt_ss, lt_rs, ld_ss, ld_rs,
    t_ss, t_rs, d_ss, d_rs, s_ss, s_rs,
):
    d = lax.axis_index("dp")
    t = lax.axis_index("tensor")
    z, xh = t // 2, t % 2
    way = 1 - 2 * (d % 2)
    owners = [lax.rem(z + way * step + RING, RING) for step in AWAY]
    forward = (d, lax.rem(z + way + RING, RING) * 2 + xh)
    backward = (d, lax.rem(z - way + RING, RING) * 2 + xh)
    partner = (d, z * 2 + 1 - xh)
    def send(src, dst, ss, rs, device):
        pltpu.make_async_remote_copy(
            src_ref=src, dst_ref=dst, send_sem=ss, recv_sem=rs, device_id=device, device_id_type=MESH
        ).start()

    def landed(ref, sem):
        pltpu.make_async_copy(ref, ref, sem).wait()

    def along(steps):
        return lax.rem(z + steps + RING, RING)

    barrier = pltpu.get_barrier_semaphore()
    near = [(d, along(way * steps) * 2 + side) for steps in (1, -1) for side in range(2)]
    near += [partner] + [(lax.rem(d + k, GROUP), t) for k in range(1, GROUP)]

    def greet(devices):
        for device in devices:
            pl.semaphore_signal(barrier, inc=1, device_id=device, device_id_type=MESH)

    def load(i, half):
        start = pl.multiple_of((half * GROUP + 2 * owners[i]) * SEQ, 2 * SEQ)
        for k, source in enumerate((in_one, grad_one, in_two, grad_two)):
            pltpu.make_async_copy(
                source.at[:, pl.ds(start, 2 * SEQ)],
                tok.at[k, :, pl.ds(start, 2 * SEQ)],
                in_sem.at[i, half],
            ).start()

    greet(near[:5])
    for k, weight in enumerate((w_in_one, w_out_one, w_in_two, w_out_two)):
        pltpu.make_async_copy(weight, weights.at[k], w_sem.at[0]).start()
    load(0, 1)
    load(0, 0)
    greet(near[5:])
    for i in (1, 2):
        load(i, 1)
        load(i, 0)
    pltpu.make_async_copy(asked, query, q_sem.at[0]).start()
    landed(weights, w_sem.at[0])

    def project(i, half):
        first = half * GROUP + 2 * owners[i]
        start = pl.multiple_of(first * SEQ, 2 * SEQ)
        landed(tok.at[:, :, pl.ds(start, 2 * SEQ)], in_sem.at[i, half])
        for k in range(4):
            both = jnp.dot(
                weights[k],
                tok[k, :, pl.ds(start, 2 * SEQ)],
                preferred_element_type=jnp.float32,
            )
            span = slice(k % 2 * RANK, (k % 2 + 1) * RANK)
            part[first, k // 2, span, :] = both[:, :SEQ]
            part[first + 1, k // 2, span, :] = both[:, SEQ:]

    def own(half, owner, side):
        index = half * GROUP + 2 * owner + side
        return [part[index, 0], part[index, 1]]

    def ring_a(i):
        for side in range(2):
            total = own(0, owners[i], side)
            if i >= 2:
                landed(a_got.at[i - 2, side], a_rs.at[i - 2, side])
                total = add(total, decode(a_got.at[i - 2, side]))
            encode(a_out.at[i, side], total)
            lane, to = side, forward if i % 2 == 0 else backward
            if i >= 5:
                lane, to = xh, (d, along(way if i % 2 == 0 else -way) * 2 + side)
            send(a_out.at[i, side], a_got.at[i, lane], a_ss.at[0], a_rs.at[i, lane], to)

    def pair(i):
        encode(x_out.at[i], own(1, owners[i], 1 - xh))
        send(x_out.at[i], x_got.at[i], x_ss.at[0], x_rs.at[i], partner)

    def ring_b(i):
        landed(x_got.at[i], x_rs.at[i])
        total = add(own(1, owners[i], xh), decode(x_got.at[i]))
        if i >= 2:
            landed(b_got.at[i - 2], b_rs.at[i - 2])
            total = add(total, decode(b_got.at[i - 2]))
        encode(b_out.at[i], total)
        send(
            b_out.at[i], b_got.at[i], b_ss.at[0], b_rs.at[i], forward if i % 2 == 0 else backward
        )

    def constants():
        at_row = lax.broadcasted_iota(jnp.int32, (GROUP * 32, GROUP * 32), 0)
        at_col = lax.broadcasted_iota(jnp.int32, (GROUP * 32, GROUP * 32), 1)
        mirrored = (at_row % 16) * 32 + (at_row // 16 % 2) * 16 + at_row // 32
        swap[...] = jnp.where(at_col == mirrored, 1.0, 0.0).astype(jnp.bfloat16)
        landed(query, q_sem.at[0])
        row = lax.broadcasted_iota(jnp.int32, pick.shape, 0)
        example = (row // 32 % 8 * 2 + row // 256) * 32 + row % 32
        pick[...] = jnp.where(example == query[...], 1.0, 0.0).astype(jnp.bfloat16)
        score_out[...] = jnp.zeros_like(score_out)

    def first(i):
        project(i, 1)
        if i == 0:
            pl.semaphore_wait(barrier, len(near))
        pair(i)

    first(0)
    for i in range(RING + 1):
        if i < RING:
            if i + 3 < RING:
                load(i + 3, 1)
                load(i + 3, 0)
            project(i, 0)
            if i < 2:
                ring_a(i)
            if i + 1 < RING:
                first(i + 1)
            if 2 <= i < RING - 1:
                ring_a(i)
            if i == RING - 1:
                encode(x_out.at[RING], own(0, z, 1 - xh))
                send(x_out.at[RING], x_got.at[RING], x_ss.at[0], x_rs.at[RING], partner)
                constants()
        if i >= 2:
            ring_b(i - 2)

    def features(half, sums):
        for layer in range(2):
            outer = lax.dot_general(
                sums[layer], sums[layer], (((1,), (1,)), ((), ())),
                precision=lax.Precision.HIGHEST, preferred_element_type=jnp.float32,
            )
            scaled = outer[RANK:, :] / jnp.float32(math.sqrt(SEQ))
            square[...] = scaled.astype(jnp.bfloat16).astype(jnp.float32)
            for pair_of in range(2):
                even = square[pl.ds(2 * pair_of, GROUP, stride=4), :]
                odd = square[pl.ds(2 * pair_of + 1, GROUP, stride=4), :]
                slices[pl.ds(half * 4 + layer * 2 + pair_of, GROUP, stride=8), :] = jnp.concatenate(
                    [even[:, :RANK], odd[:, :RANK]], 1
                )

    for i in (5, 6):
        landed(b_got.at[i], b_rs.at[i])
    landed(x_got.at[RING - 1], x_rs.at[RING - 1])
    total = add(own(1, z, xh), decode(x_got.at[RING - 1]))
    for i in (5, 6):
        total = add(total, decode(b_got.at[i]))
    features(1, total)
    landed(x_got.at[RING], x_rs.at[RING])
    total = add(own(0, z, xh), decode(x_got.at[RING]))
    for i in (5, 6):
        for side in range(2):
            landed(a_got.at[i, side], a_rs.at[i, side])
            total = add(total, decode(a_got.at[i, side]))
    features(0, total)

    place = d % 2 * 8 + d // 2

    def tile(index):
        return pl.ds(pl.multiple_of(8 * index, 8), 8)

    for k in sorted(range(1, GROUP), key=lambda k: abs(k - 8)):
        to = lax.rem(t + k, GROUP)
        send(slices.at[tile(to)], land_t.at[tile(t)], lt_ss.at[0], lt_rs.at[0], (d, to))
    for k in range(1, GROUP):
        to = lax.rem(d + k, GROUP)
        send(slices.at[tile(to)], land_d.at[tile(place)], ld_ss.at[0], ld_rs.at[0], (to, t))
    land_t[tile(t), :] = slices[tile(t), :]
    land_d[tile(place), :] = slices[tile(d), :]

    def gather(land, block, rs):
        landed(land.at[pl.ds(0, 8 * (GROUP - 1))], rs.at[0])
        for half in range(2):
            lanes = [land[pl.ds(half * 4 + k, GROUP, stride=8), :] for k in range(4)]
            block[half * GROUP : (half + 1) * GROUP, :] = jnp.concatenate(lanes, 1).astype(
                jnp.bfloat16
            )

    gather(land_t, rows.at[place], lt_rs)
    for k in range(1, 8):
        send(rows.at[place], rows.at[place], t_ss.at[0], t_rs.at[0], (lax.rem(d + 2 * k, GROUP), t))

    gather(land_d, cols.at[t], ld_rs)
    for steps in (2, 1, 0):
        for flip in range(2):
            for sign in (1, -1) if steps else (1,):
                if steps or flip:
                    to = along(sign * steps) * 2 + (1 - xh if flip else xh)
                    sem = flip if steps == 2 else 2
                    send(cols.at[t], cols.at[t], d_ss.at[0], d_rs.at[sem], (d, to))

    landed(rows.at[pl.ds(0, 7)], t_rs.at[0])
    block = pl.ds(d % 2 * 8, 8)
    sibling = (d + 1 - 2 * (d % 2), t)
    send(rows.at[block], rows.at[block], t_ss.at[1], t_rs.at[1], sibling)

    for flip in range(2):
        landed(cols.at[pl.ds(0, 2)], d_rs.at[flip])
        for held, steps in ((-2 * way, 2 * way), (-2 * way, way), (2 * way, -way)):
            block = along(held) * 2 + (1 - xh if flip else xh)
            to = along(steps) * 2 + xh
            send(cols.at[block], cols.at[block], d_ss.at[1], d_rs.at[3], (d, to))

    landed(rows.at[pl.ds(0, 8)], t_rs.at[1])
    mine = rows[place]
    all_rows = rows[...].reshape(GROUP * 32, 4 * LANES)
    query_feat = lax.dot_general(
        pick[...], all_rows, (((0,), (0,)), ((), ())), preferred_element_type=jnp.float32
    ).astype(jnp.bfloat16)
    partial_scores = lax.dot_general(
        query_feat, mine, (((1,), (1,)), ((), ())), preferred_element_type=jnp.float32
    )
    for k in range(GROUP):
        score_out[8 * k : 8 * k + 4, 0:32] = partial_scores[4 * k : 4 * k + 4, :]
    for k in sorted(range(1, GROUP), key=lambda k: abs(k - 8)):
        to = lax.rem(t + k, GROUP)
        send(score_out.at[tile(to)], score_got.at[tile(t)], s_ss.at[0], s_rs.at[0], (d, to))
    score_got[tile(t), :] = score_out[tile(t), :]
    turned[...] = lax.dot_general(
        all_rows, swap[...], (((0,), (0,)), ((), ())), preferred_element_type=jnp.float32
    ).astype(jnp.bfloat16)

    landed(cols.at[pl.ds(0, 5)], d_rs.at[2])
    landed(cols.at[pl.ds(0, 6)], d_rs.at[3])
    all_cols = cols[...].reshape(GROUP * 32, 4 * LANES)
    for layer in range(2):
        span = slice(layer * 2 * LANES, (layer + 1) * 2 * LANES)
        gram[layer] = jnp.dot(
            turned[span, :], all_cols[:, span], preferred_element_type=jnp.float32
        ) * jnp.float32(1.0 / 512)

    landed(score_got.at[pl.ds(0, 8 * (GROUP - 1))], s_rs.at[0])
    total = score_got[0:8, :]
    for k in range(1, GROUP):
        total = total + score_got[8 * k : 8 * k + 8, :]
    scores[...] = total[0:4, 0:32] / jnp.float32(math.sqrt(2 * RANK * RANK))

    tiles = pl.ds(0, 8 * (GROUP - 1))
    for ref, sem in (
        (a_out, a_ss.at[0]),
        (b_out, b_ss.at[0]),
        (x_out, x_ss.at[0]),
        (land_t.at[tiles], lt_ss.at[0]),
        (land_d.at[tiles], ld_ss.at[0]),
        (rows.at[pl.ds(0, 7)], t_ss.at[0]),
        (rows.at[pl.ds(0, 8)], t_ss.at[1]),
        (cols.at[pl.ds(0, 9)], d_ss.at[0]),
        (cols.at[pl.ds(0, 6)], d_ss.at[1]),
        (score_got.at[tiles], s_ss.at[0]),
    ):
        landed(ref, sem)


def local(*args):
    tokens, width = args[0].shape
    query = args[-1].reshape(1, -1)
    dma = pltpu.SemaphoreType.DMA
    f32, bf16, i16 = jnp.float32, jnp.bfloat16, jnp.int16
    vmem = pltpu.VMEM
    scratch = [
        vmem((4, width, tokens), bf16),
        vmem((4, RANK, width), bf16),
        vmem(query.shape, jnp.int32),
        vmem((tokens // SEQ, 2, LANES, SEQ), f32),
        vmem((7, 2, PACK, LANES), i16),
        vmem((7, 2, PACK, LANES), i16),
        vmem((7, PACK, LANES), i16),
        vmem((7, PACK, LANES), i16),
        vmem((RING + 1, PACK, LANES), i16),
        vmem((RING + 1, PACK, LANES), i16),
        vmem((RANK, LANES), f32),
        vmem((8 * GROUP, LANES), f32),
        vmem((8 * GROUP, LANES), f32),
        vmem((8 * GROUP, LANES), f32),
        vmem((GROUP, 32, 4 * LANES), bf16),
        vmem((GROUP, 32, 4 * LANES), bf16),
        vmem((GROUP * 32, GROUP * 32), bf16),
        vmem((GROUP * 32, query.shape[1]), bf16),
        vmem((4 * LANES, GROUP * 32), bf16),
        vmem((8 * GROUP, LANES), f32),
        vmem((8 * GROUP, LANES), f32),
        dma((RING, 2)), dma((1,)), dma((1,)),
        dma((1,)), dma((7, 2)),
        dma((1,)), dma((7,)),
        dma((1,)), dma((RING + 1,)),
        dma((1,)), dma((1,)),
        dma((1,)), dma((1,)),
        dma((2,)), dma((2,)),
        dma((2,)), dma((4,)),
        dma((1,)), dma((1,)),
    ]
    in_hbm = pl.BlockSpec(memory_space=pltpu.HBM)
    in_vmem = pl.BlockSpec(memory_space=pltpu.VMEM)
    return pl.pallas_call(
        kernel,
        out_shape=(
            jax.ShapeDtypeStruct((2, 256, 256), f32),
            jax.ShapeDtypeStruct((4, 32), f32),
        ),
        in_specs=[in_hbm] * 9,
        out_specs=(in_vmem, in_vmem),
        scratch_shapes=scratch,
        compiler_params=pltpu.CompilerParams(
            collective_id=0, has_side_effects=True, vmem_limit_bytes=58 << 20
        ),
    )(*[arg.T for arg in args[:-1]], query)


def solution(mesh):
    in_specs = (
        P("dp", "tensor"),
        P("dp", "tensor"),
        P("dp", "tensor"),
        P("dp", "tensor"),
        P("tensor", None),
        P("tensor", None),
        P("tensor", None),
        P("tensor", None),
        P(),
    )
    out_specs = (P(None, "tensor", "dp"), P("tensor", "dp"))
    return jax.shard_map(local, mesh=mesh, in_specs=in_specs, out_specs=out_specs, check_vma=False)
```

```python
import math

import jax
import jax.numpy as jnp
from jax import lax
from jax.experimental import pallas as pl
from jax.experimental.pallas import tpu as pltpu
from jax.sharding import PartitionSpec as P

SEQ = 128
RANK = 64
GROUP = 16
RING = 8
LANES = 128
PACK = 4 * RANK + 16
MESH = pl.DeviceIdType.MESH
AWAY = (4, -3, 3, -2, 2, -1, 1, 0)


def encode(dst, layers):
    keys = []
    for which, values in enumerate(layers):
        for side in range(2):
            some = values[side * RANK : (side + 1) * RANK]
            top = jnp.max(jnp.abs(some), axis=0, keepdims=True)
            key = jnp.ceil(8.0 * jnp.log2(jnp.maximum(top, 1e-30)) + 0.1)
            scaled = jnp.round(some * jnp.exp2(15.0 - key * 0.125))
            start = (2 * which + side) * RANK
            dst[start : start + RANK, :] = scaled.astype(jnp.int32).astype(jnp.int16)
            keys.append(key)
    row = lax.broadcasted_iota(jnp.int32, (16, SEQ), 0)
    both = jnp.where(row < 4, keys[0], keys[1])
    both = jnp.where(row < 8, both, jnp.where(row < 12, keys[2], keys[3]))
    dst[4 * RANK : PACK, :] = both.astype(jnp.int32).astype(jnp.int16)


def decode(src):
    keys = src[4 * RANK : PACK, :].astype(jnp.int32).astype(jnp.float32)
    out = []
    for which in range(4):
        step = jnp.exp2(keys[4 * which : 4 * which + 1, :] * 0.125 - 15.0)
        whole = src[which * RANK : (which + 1) * RANK, :].astype(jnp.int32).astype(jnp.float32)
        out.append(whole * step)
    return [jnp.concatenate(out[:2], 0), jnp.concatenate(out[2:], 0)]


def add(one, two):
    return [a + b for a, b in zip(one, two)]


def kernel(
    in_one, grad_one, in_two, grad_two, w_in_one, w_out_one, w_in_two, w_out_two, asked,
    gram, scores,
    tok, weights, query, part, a_out, a_got, b_out, b_got, x_out, x_got, square, slices, land_t, land_d,
    rows, cols, swap, pick, turned, result, query_out, query_got, score_out, score_got,
    in_sem, w_sem, q_sem, a_ss, a_rs, b_ss, b_rs, x_ss, x_rs, lt_ss, lt_rs, ld_ss, ld_rs,
    t_ss, t_rs, d_ss, d_rs, s_ss, s_rs, qs_sem, g_sem,
):
    d = lax.axis_index("dp")
    t = lax.axis_index("tensor")
    z, xh = t // 2, t % 2
    way = 1 - 2 * (d % 2)
    owners = [lax.rem(z + way * step + RING, RING) for step in AWAY]
    forward = (d, lax.rem(z + way + RING, RING) * 2 + xh)
    backward = (d, lax.rem(z - way + RING, RING) * 2 + xh)
    partner = (d, z * 2 + 1 - xh)
    def send(src, dst, ss, rs, device):
        pltpu.make_async_remote_copy(
            src_ref=src, dst_ref=dst, send_sem=ss, recv_sem=rs, device_id=device, device_id_type=MESH
        ).start()

    def landed(ref, sem):
        pltpu.make_async_copy(ref, ref, sem).wait()

    def along(steps):
        return lax.rem(z + steps + RING, RING)

    barrier = pltpu.get_barrier_semaphore()
    near = [(d, along(way * steps) * 2 + side) for steps in (1, -1) for side in range(2)]
    near += [partner] + [(lax.rem(d + k, GROUP), t) for k in range(1, GROUP)]

    def greet(devices):
        for device in devices:
            pl.semaphore_signal(barrier, inc=1, device_id=device, device_id_type=MESH)

    def load(i, half):
        start = pl.multiple_of((half * GROUP + 2 * owners[i]) * SEQ, 2 * SEQ)
        for k, source in enumerate((in_one, grad_one, in_two, grad_two)):
            pltpu.make_async_copy(
                source.at[:, pl.ds(start, 2 * SEQ)],
                tok.at[k, :, pl.ds(start, 2 * SEQ)],
                in_sem.at[i, half],
            ).start()

    greet(near[:5])
    for k, weight in enumerate((w_in_one, w_out_one, w_in_two, w_out_two)):
        pltpu.make_async_copy(weight, weights.at[k], w_sem.at[0]).start()
    load(0, 1)
    load(0, 0)
    greet(near[5:])
    landed(weights, w_sem.at[0])

    def project(i, half):
        first = half * GROUP + 2 * owners[i]
        start = pl.multiple_of(first * SEQ, 2 * SEQ)
        landed(tok.at[:, :, pl.ds(start, 2 * SEQ)], in_sem.at[i, half])
        for k in range(4):
            both = jnp.dot(
                weights[k],
                tok[k, :, pl.ds(start, 2 * SEQ)],
                preferred_element_type=jnp.float32,
            )
            span = slice(k % 2 * RANK, (k % 2 + 1) * RANK)
            part[first, k // 2, span, :] = both[:, :SEQ]
            part[first + 1, k // 2, span, :] = both[:, SEQ:]

    def own(half, owner, side):
        index = half * GROUP + 2 * owner + side
        return [part[index, 0], part[index, 1]]

    def ring_a(i):
        for side in range(2):
            total = own(0, owners[i], side)
            if i >= 2:
                landed(a_got.at[i - 2, side], a_rs.at[i - 2, side])
                total = add(total, decode(a_got.at[i - 2, side]))
            encode(a_out.at[i, side], total)
            lane, to = side, forward if i % 2 == 0 else backward
            if i >= 5:
                lane, to = xh, (d, along(way if i % 2 == 0 else -way) * 2 + side)
            send(a_out.at[i, side], a_got.at[i, lane], a_ss.at[0], a_rs.at[i, lane], to)

    def pair(i):
        encode(x_out.at[i], own(1, owners[i], 1 - xh))
        send(x_out.at[i], x_got.at[i], x_ss.at[0], x_rs.at[i], partner)

    def ring_b(i):
        landed(x_got.at[i], x_rs.at[i])
        total = add(own(1, owners[i], xh), decode(x_got.at[i]))
        if i >= 2:
            landed(b_got.at[i - 2], b_rs.at[i - 2])
            total = add(total, decode(b_got.at[i - 2]))
        encode(b_out.at[i], total)
        send(
            b_out.at[i], b_got.at[i], b_ss.at[0], b_rs.at[i], forward if i % 2 == 0 else backward
        )

    def constants():
        at_row = lax.broadcasted_iota(jnp.int32, (GROUP * 32, GROUP * 32), 0)
        at_col = lax.broadcasted_iota(jnp.int32, (GROUP * 32, GROUP * 32), 1)
        mirrored = (at_row % 16) * 32 + (at_row // 16 % 2) * 16 + at_row // 32
        swap[...] = jnp.where(at_col == mirrored, 1.0, 0.0).astype(jnp.bfloat16)
        landed(query, q_sem.at[0])
        row = lax.broadcasted_iota(jnp.int32, pick.shape, 0)
        example = (row // 32 % 8 * 2 + row // 256) * 32 + row % 32
        pick[...] = jnp.where(example == query[...], 1.0, 0.0).astype(jnp.bfloat16)
        score_out[...] = jnp.zeros_like(score_out)

    def first(i):
        project(i, 1)
        if i == 0:
            pl.semaphore_wait(barrier, len(near))
        pair(i)

    def loads(*which):
        for i, half in which:
            load(i, half)

    first(0)
    loads((1, 1), (1, 0), (2, 1), (3, 1))
    project(0, 0)
    ring_a(0)
    loads((2, 0), (4, 1))
    first(1)
    project(1, 0)
    ring_a(1)
    loads((3, 0), (5, 1))
    first(2)
    loads((4, 0), (6, 1))
    first(3)
    loads((5, 0), (7, 1))
    pltpu.make_async_copy(asked, query, q_sem.at[0]).start()
    project(2, 0)
    ring_b(0)
    for i in range(2, RING - 1):
        ring_a(i)
        ring_b(i - 1)
        if i == 2:
            loads((6, 0), (7, 0))
        if i + 2 < RING:
            first(i + 2)
        if i < RING - 2:
            project(i + 1, 0)
        if i == RING - 3:
            project(RING - 1, 0)
            encode(x_out.at[RING], own(0, z, 1 - xh))
            send(x_out.at[RING], x_got.at[RING], x_ss.at[0], x_rs.at[RING], partner)
    ring_b(RING - 2)
    constants()

    def features(half, sums):
        for layer in range(2):
            outer = lax.dot_general(
                sums[layer], sums[layer], (((1,), (1,)), ((), ())),
                precision=lax.Precision.HIGHEST, preferred_element_type=jnp.float32,
            )
            scaled = outer[RANK:, :] / jnp.float32(math.sqrt(SEQ))
            square[...] = scaled.astype(jnp.bfloat16).astype(jnp.float32)
            for pair_of in range(2):
                even = square[pl.ds(2 * pair_of, GROUP, stride=4), :]
                odd = square[pl.ds(2 * pair_of + 1, GROUP, stride=4), :]
                slices[pl.ds(half * 4 + layer * 2 + pair_of, GROUP, stride=8), :] = jnp.concatenate(
                    [even[:, :RANK], odd[:, :RANK]], 1
                )

    for i in (5, 6):
        landed(b_got.at[i], b_rs.at[i])
    landed(x_got.at[RING - 1], x_rs.at[RING - 1])
    total = add(own(1, z, xh), decode(x_got.at[RING - 1]))
    for i in (5, 6):
        total = add(total, decode(b_got.at[i]))
    features(1, total)
    landed(x_got.at[RING], x_rs.at[RING])
    total = add(own(0, z, xh), decode(x_got.at[RING]))
    for i in (5, 6):
        for side in range(2):
            landed(a_got.at[i, side], a_rs.at[i, side])
            total = add(total, decode(a_got.at[i, side]))
    features(0, total)

    place = d % 2 * 8 + d // 2

    def tile(index):
        return pl.ds(pl.multiple_of(8 * index, 8), 8)

    for k in sorted(range(1, GROUP), key=lambda k: abs(k - 8)):
        to = lax.rem(t + k, GROUP)
        send(slices.at[tile(to)], land_t.at[tile(t)], lt_ss.at[0], lt_rs.at[0], (d, to))
    for k in range(1, GROUP):
        to = lax.rem(d + k, GROUP)
        send(slices.at[tile(to)], land_d.at[tile(place)], ld_ss.at[0], ld_rs.at[0], (to, t))
    land_t[tile(t), :] = slices[tile(t), :]
    land_d[tile(place), :] = slices[tile(d), :]

    def gather(land, block, rs):
        landed(land.at[pl.ds(0, 8 * (GROUP - 1))], rs.at[0])
        for half in range(2):
            lanes = [land[pl.ds(half * 4 + k, GROUP, stride=8), :] for k in range(4)]
            block[half * GROUP : (half + 1) * GROUP, :] = jnp.concatenate(lanes, 1).astype(
                jnp.bfloat16
            )

    gather(land_t, rows.at[place], lt_rs)
    for k in range(1, 8):
        send(rows.at[place], rows.at[place], t_ss.at[0], t_rs.at[0], (lax.rem(d + 2 * k, GROUP), t))

    gather(land_d, cols.at[t], ld_rs)
    for steps in (2, 1, 0):
        for flip in range(2):
            for sign in (1, -1) if steps else (1,):
                if steps or flip:
                    to = along(sign * steps) * 2 + (1 - xh if flip else xh)
                    sem = flip if steps == 2 else 2
                    send(cols.at[t], cols.at[t], d_ss.at[0], d_rs.at[sem], (d, to))

    def further(flip):
        landed(cols.at[pl.ds(0, 2)], d_rs.at[flip])
        for held, steps in ((-2 * way, 2 * way), (-2 * way, way), (2 * way, -way)):
            block = along(held) * 2 + (1 - xh if flip else xh)
            to = along(steps) * 2 + xh
            send(cols.at[block], cols.at[block], d_ss.at[1], d_rs.at[3], (d, to))

    further(0)
    landed(rows.at[pl.ds(0, 7)], t_rs.at[0])
    side = d % 2
    block = pl.ds(side * 8, 8)
    sibling = (d + 1 - 2 * side, t)
    half_pick = pick[pl.ds(pl.multiple_of(side * 256, 256), 256), :]
    half_rows = rows[block].reshape(256, 4 * LANES)
    query_out[...] = lax.dot_general(
        half_pick, half_rows, (((0,), (0,)), ((), ())), preferred_element_type=jnp.float32
    ).astype(jnp.bfloat16)
    send(query_out, query_got, qs_sem.at[0], qs_sem.at[1], sibling)
    send(rows.at[block], rows.at[block], t_ss.at[1], t_rs.at[1], sibling)

    landed(query_got, qs_sem.at[1])
    partial_scores = lax.dot_general(
        query_out[...] + query_got[...],
        rows[place],
        (((1,), (1,)), ((), ())),
        preferred_element_type=jnp.float32,
    )
    for k in range(GROUP):
        score_out[8 * k : 8 * k + 4, 0:32] = partial_scores[4 * k : 4 * k + 4, :]
    for k in sorted(range(1, GROUP), key=lambda k: abs(k - 8)):
        to = lax.rem(t + k, GROUP)
        send(score_out.at[tile(to)], score_got.at[tile(t)], s_ss.at[0], s_rs.at[0], (d, to))
    further(1)
    score_got[tile(t), :] = score_out[tile(t), :]
    landed(rows.at[pl.ds(0, 8)], t_rs.at[1])
    all_rows = rows[...].reshape(GROUP * 32, 4 * LANES)
    turned[...] = lax.dot_general(
        all_rows, swap[...], (((0,), (0,)), ((), ())), preferred_element_type=jnp.float32
    ).astype(jnp.bfloat16)

    landed(cols.at[pl.ds(0, 5)], d_rs.at[2])
    landed(cols.at[pl.ds(0, 6)], d_rs.at[3])
    all_cols = cols[...].reshape(GROUP * 32, 4 * LANES)
    for layer in range(2):
        span = slice(layer * 2 * LANES, (layer + 1) * 2 * LANES)
        result[layer] = jnp.dot(
            turned[span, :], all_cols[:, span], preferred_element_type=jnp.float32
        ) * jnp.float32(1.0 / 512)
        pltpu.make_async_copy(result.at[layer], gram.at[layer], g_sem.at[layer]).start()

    landed(score_got.at[pl.ds(0, 8 * (GROUP - 1))], s_rs.at[0])
    total = score_got[0:8, :]
    for k in range(1, GROUP):
        total = total + score_got[8 * k : 8 * k + 8, :]
    scores[...] = total[0:4, 0:32] / jnp.float32(math.sqrt(2 * RANK * RANK))

    tiles = pl.ds(0, 8 * (GROUP - 1))
    for ref, sem in (
        (a_out, a_ss.at[0]),
        (b_out, b_ss.at[0]),
        (x_out, x_ss.at[0]),
        (land_t.at[tiles], lt_ss.at[0]),
        (land_d.at[tiles], ld_ss.at[0]),
        (rows.at[pl.ds(0, 7)], t_ss.at[0]),
        (rows.at[pl.ds(0, 8)], t_ss.at[1]),
        (cols.at[pl.ds(0, 9)], d_ss.at[0]),
        (cols.at[pl.ds(0, 6)], d_ss.at[1]),
        (score_got.at[tiles], s_ss.at[0]),
        (query_out, qs_sem.at[0]),
        (result.at[0], g_sem.at[0]),
        (result.at[1], g_sem.at[1]),
    ):
        landed(ref, sem)


def local(*args):
    tokens, width = args[0].shape
    query = args[-1].reshape(1, -1)
    dma = pltpu.SemaphoreType.DMA
    f32, bf16, i16 = jnp.float32, jnp.bfloat16, jnp.int16
    vmem = pltpu.VMEM
    scratch = [
        vmem((4, width, tokens), bf16),
        vmem((4, RANK, width), bf16),
        vmem(query.shape, jnp.int32),
        vmem((tokens // SEQ, 2, LANES, SEQ), f32),
        vmem((7, 2, PACK, LANES), i16),
        vmem((7, 2, PACK, LANES), i16),
        vmem((7, PACK, LANES), i16),
        vmem((7, PACK, LANES), i16),
        vmem((RING + 1, PACK, LANES), i16),
        vmem((RING + 1, PACK, LANES), i16),
        vmem((RANK, LANES), f32),
        vmem((8 * GROUP, LANES), f32),
        vmem((8 * GROUP, LANES), f32),
        vmem((8 * GROUP, LANES), f32),
        vmem((GROUP, 32, 4 * LANES), bf16),
        vmem((GROUP, 32, 4 * LANES), bf16),
        vmem((GROUP * 32, GROUP * 32), bf16),
        vmem((GROUP * 32, query.shape[1]), bf16),
        vmem((4 * LANES, GROUP * 32), bf16),
        vmem((2, 256, 256), f32),
        vmem((query.shape[1], 4 * LANES), bf16),
        vmem((query.shape[1], 4 * LANES), bf16),
        vmem((8 * GROUP, LANES), f32),
        vmem((8 * GROUP, LANES), f32),
        dma((RING, 2)), dma((1,)), dma((1,)),
        dma((1,)), dma((7, 2)),
        dma((1,)), dma((7,)),
        dma((1,)), dma((RING + 1,)),
        dma((1,)), dma((1,)),
        dma((1,)), dma((1,)),
        dma((2,)), dma((2,)),
        dma((2,)), dma((4,)),
        dma((1,)), dma((1,)),
        dma((2,)), dma((2,)),
    ]
    in_hbm = pl.BlockSpec(memory_space=pltpu.HBM)
    in_vmem = pl.BlockSpec(memory_space=pltpu.VMEM)
    return pl.pallas_call(
        kernel,
        out_shape=(
            jax.ShapeDtypeStruct((2, 256, 256), f32),
            jax.ShapeDtypeStruct((4, 32), f32),
        ),
        in_specs=[in_hbm] * 9,
        out_specs=(in_hbm, in_vmem),
        scratch_shapes=scratch,
        compiler_params=pltpu.CompilerParams(
            collective_id=0, has_side_effects=True, vmem_limit_bytes=58 << 20
        ),
    )(*[arg.T for arg in args[:-1]], query)


def solution(mesh):
    in_specs = (
        P("dp", "tensor"),
        P("dp", "tensor"),
        P("dp", "tensor"),
        P("dp", "tensor"),
        P("tensor", None),
        P("tensor", None),
        P("tensor", None),
        P("tensor", None),
        P(),
    )
    out_specs = (P(None, "tensor", "dp"), P("tensor", "dp"))
    return jax.shard_map(local, mesh=mesh, in_specs=in_specs, out_specs=out_specs, check_vma=False)
```

```python
import math

import jax
import jax.numpy as jnp
from jax import lax
from jax.experimental import pallas as pl
from jax.experimental.pallas import tpu as pltpu
from jax.sharding import PartitionSpec as P

SEQ = 128
RANK = 64
GROUP = 16
RING = 8
LANES = 128
PACK = 4 * RANK + 16
MESH = pl.DeviceIdType.MESH
AWAY = (4, -3, 3, -2, 2, -1, 1, 0)


def encode(dst, layers):
    keys = []
    for which, values in enumerate(layers):
        for side in range(2):
            some = values[side * RANK : (side + 1) * RANK]
            top = jnp.max(jnp.abs(some), axis=0, keepdims=True)
            key = jnp.ceil(8.0 * jnp.log2(jnp.maximum(top, 1e-30)) + 0.1)
            scaled = jnp.round(some * jnp.exp2(15.0 - key * 0.125))
            start = (2 * which + side) * RANK
            dst[start : start + RANK, :] = scaled.astype(jnp.int32).astype(jnp.int16)
            keys.append(key)
    row = lax.broadcasted_iota(jnp.int32, (16, SEQ), 0)
    both = jnp.where(row < 4, keys[0], keys[1])
    both = jnp.where(row < 8, both, jnp.where(row < 12, keys[2], keys[3]))
    dst[4 * RANK : PACK, :] = both.astype(jnp.int32).astype(jnp.int16)


def decode(src):
    keys = src[4 * RANK : PACK, :].astype(jnp.int32).astype(jnp.float32)
    out = []
    for which in range(4):
        step = jnp.exp2(keys[4 * which : 4 * which + 1, :] * 0.125 - 15.0)
        whole = src[which * RANK : (which + 1) * RANK, :].astype(jnp.int32).astype(jnp.float32)
        out.append(whole * step)
    return [jnp.concatenate(out[:2], 0), jnp.concatenate(out[2:], 0)]


def add(one, two):
    return [a + b for a, b in zip(one, two)]


def kernel(
    in_one, grad_one, in_two, grad_two, w_in_one, w_out_one, w_in_two, w_out_two, asked,
    gram, scores,
    tok, weights, query, part, a_out, a_got, b_out, b_got, x_out, x_got, square, slices, land_t, land_d,
    rows, cols, swap, pick, turned, result, query_out, query_got, score_out, score_got,
    in_sem, w_sem, q_sem, a_ss, a_rs, b_ss, b_rs, x_ss, x_rs, lt_ss, lt_rs, ld_ss, ld_rs,
    t_ss, t_rs, d_ss, d_rs, s_ss, s_rs, qs_sem, g_sem,
):
    d = lax.axis_index("dp")
    t = lax.axis_index("tensor")
    z, xh = t // 2, t % 2
    way = 1 - 2 * (d % 2)
    owners = [lax.rem(z + way * step + RING, RING) for step in AWAY]
    forward = (d, lax.rem(z + way + RING, RING) * 2 + xh)
    backward = (d, lax.rem(z - way + RING, RING) * 2 + xh)
    partner = (d, z * 2 + 1 - xh)
    def send(src, dst, ss, rs, device):
        pltpu.make_async_remote_copy(
            src_ref=src, dst_ref=dst, send_sem=ss, recv_sem=rs, device_id=device, device_id_type=MESH
        ).start()

    def landed(ref, sem):
        pltpu.make_async_copy(ref, ref, sem).wait()

    def along(steps):
        return lax.rem(z + steps + RING, RING)

    barrier = pltpu.get_barrier_semaphore()
    near = [(d, along(way * steps) * 2 + side) for steps in (1, -1) for side in range(2)]
    near += [partner] + [(lax.rem(d + k, GROUP), t) for k in range(1, GROUP)]

    def greet(devices):
        for device in devices:
            pl.semaphore_signal(barrier, inc=1, device_id=device, device_id_type=MESH)

    def load(i, half):
        start = pl.multiple_of((half * GROUP + 2 * owners[i]) * SEQ, 2 * SEQ)
        for k, source in enumerate((in_one, grad_one, in_two, grad_two)):
            pltpu.make_async_copy(
                source.at[:, pl.ds(start, 2 * SEQ)],
                tok.at[k, :, pl.ds(start, 2 * SEQ)],
                in_sem.at[i, half],
            ).start()

    greet(near[:5])
    for k, weight in enumerate((w_in_one, w_out_one, w_in_two, w_out_two)):
        pltpu.make_async_copy(weight, weights.at[k], w_sem.at[0]).start()
    load(0, 0)
    load(0, 1)
    greet(near[5:])
    landed(weights, w_sem.at[0])

    def project(i, half):
        first = half * GROUP + 2 * owners[i]
        start = pl.multiple_of(first * SEQ, 2 * SEQ)
        landed(tok.at[:, :, pl.ds(start, 2 * SEQ)], in_sem.at[i, half])
        for k in range(4):
            both = jnp.dot(
                weights[k],
                tok[k, :, pl.ds(start, 2 * SEQ)],
                preferred_element_type=jnp.float32,
            )
            span = slice(k % 2 * RANK, (k % 2 + 1) * RANK)
            part[first, k // 2, span, :] = both[:, :SEQ]
            part[first + 1, k // 2, span, :] = both[:, SEQ:]

    def own(half, owner, side):
        index = half * GROUP + 2 * owner + side
        return [part[index, 0], part[index, 1]]

    def ring_a(i):
        for side in range(2):
            total = own(0, owners[i], side)
            if i >= 2:
                landed(a_got.at[i - 2, side], a_rs.at[i - 2, side])
                total = add(total, decode(a_got.at[i - 2, side]))
            encode(a_out.at[i, side], total)
            lane, to = side, forward if i % 2 == 0 else backward
            if i >= 5:
                lane, to = xh, (d, along(way if i % 2 == 0 else -way) * 2 + side)
            send(a_out.at[i, side], a_got.at[i, lane], a_ss.at[0], a_rs.at[i, lane], to)

    def pair(i):
        encode(x_out.at[i], own(1, owners[i], 1 - xh))
        send(x_out.at[i], x_got.at[i], x_ss.at[0], x_rs.at[i], partner)

    def ring_b(i):
        landed(x_got.at[i], x_rs.at[i])
        total = add(own(1, owners[i], xh), decode(x_got.at[i]))
        if i >= 2:
            landed(b_got.at[i - 2], b_rs.at[i - 2])
            total = add(total, decode(b_got.at[i - 2]))
        encode(b_out.at[i], total)
        send(
            b_out.at[i], b_got.at[i], b_ss.at[0], b_rs.at[i], forward if i % 2 == 0 else backward
        )

    def constants():
        at_row = lax.broadcasted_iota(jnp.int32, (GROUP * 32, GROUP * 32), 0)
        at_col = lax.broadcasted_iota(jnp.int32, (GROUP * 32, GROUP * 32), 1)
        mirrored = (at_row % 16) * 32 + (at_row // 16 % 2) * 16 + at_row // 32
        swap[...] = jnp.where(at_col == mirrored, 1.0, 0.0).astype(jnp.bfloat16)
        landed(query, q_sem.at[0])
        row = lax.broadcasted_iota(jnp.int32, pick.shape[::-1], 0)
        example = (row // 32 % 8 * 2 + row // 256) * 32 + row % 32
        pick[...] = jnp.where(example == query[...], 1.0, 0.0).T.astype(jnp.bfloat16)
        score_out[...] = jnp.zeros_like(score_out)

    def first(i):
        project(i, 1)
        pair(i)

    def loads(*which):
        for i, half in which:
            load(i, half)

    project(0, 0)
    pl.semaphore_wait(barrier, len(near))
    ring_a(0)
    first(0)
    loads((1, 0), (1, 1), (2, 1), (3, 1))
    loads((2, 0), (4, 1))
    first(1)
    project(1, 0)
    ring_a(1)
    loads((3, 0), (5, 1))
    first(2)
    loads((4, 0), (6, 1))
    first(3)
    loads((5, 0), (7, 1))
    pltpu.make_async_copy(asked, query, q_sem.at[0]).start()
    project(2, 0)
    ring_b(0)
    for i in range(2, RING - 1):
        ring_a(i)
        ring_b(i - 1)
        if i == 2:
            loads((6, 0), (7, 0))
        if i + 2 < RING:
            first(i + 2)
        if i < RING - 2:
            project(i + 1, 0)
        if i == RING - 3:
            project(RING - 1, 0)
            encode(x_out.at[RING], own(0, z, 1 - xh))
            send(x_out.at[RING], x_got.at[RING], x_ss.at[0], x_rs.at[RING], partner)
    ring_b(RING - 2)
    constants()

    def features(half, sums):
        for layer in range(2):
            outer = lax.dot_general(
                sums[layer][RANK:], sums[layer], (((1,), (1,)), ((), ())),
                precision=lax.Precision.HIGHEST, preferred_element_type=jnp.float32,
            )
            scaled = outer / jnp.float32(math.sqrt(SEQ))
            square[layer] = scaled.astype(jnp.bfloat16).astype(jnp.float32)
        for layer in range(2):
            for pair_of in range(2):
                even = square[layer, pl.ds(2 * pair_of, GROUP, stride=4), :]
                odd = square[layer, pl.ds(2 * pair_of + 1, GROUP, stride=4), :]
                slices[pl.ds(half * 4 + layer * 2 + pair_of, GROUP, stride=8), :] = jnp.concatenate(
                    [even[:, :RANK], odd[:, :RANK]], 1
                )

    for i in (5, 6):
        landed(b_got.at[i], b_rs.at[i])
    landed(x_got.at[RING - 1], x_rs.at[RING - 1])
    total = add(own(1, z, xh), decode(x_got.at[RING - 1]))
    for i in (5, 6):
        total = add(total, decode(b_got.at[i]))
    features(1, total)
    landed(x_got.at[RING], x_rs.at[RING])
    total = add(own(0, z, xh), decode(x_got.at[RING]))
    for i in (5, 6):
        for side in range(2):
            landed(a_got.at[i, side], a_rs.at[i, side])
            total = add(total, decode(a_got.at[i, side]))
    features(0, total)

    place = d % 2 * 8 + d // 2

    def tile(index):
        return pl.ds(pl.multiple_of(8 * index, 8), 8)

    for k in sorted(range(1, GROUP), key=lambda k: abs(k - 8)):
        to = lax.rem(t + k, GROUP)
        send(slices.at[tile(to)], land_t.at[tile(t)], lt_ss.at[0], lt_rs.at[0], (d, to))
    for k in range(1, GROUP):
        to = lax.rem(d + k, GROUP)
        send(slices.at[tile(to)], land_d.at[tile(place)], ld_ss.at[0], ld_rs.at[0], (to, t))
    land_t[tile(t), :] = slices[tile(t), :]
    land_d[tile(place), :] = slices[tile(d), :]

    def gather(land, block, rs):
        landed(land.at[pl.ds(0, 8 * (GROUP - 1))], rs.at[0])
        for half in range(2):
            lanes = [land[pl.ds(half * 4 + k, GROUP, stride=8), :] for k in range(4)]
            block[half * GROUP : (half + 1) * GROUP, :] = jnp.concatenate(lanes, 1).astype(
                jnp.bfloat16
            )

    gather(land_t, rows.at[place], lt_rs)
    for k in range(1, 8):
        send(rows.at[place], rows.at[place], t_ss.at[0], t_rs.at[0], (lax.rem(d + 2 * k, GROUP), t))

    gather(land_d, cols.at[t], ld_rs)
    for flip in range(2):
        for steps in (2, 1, 0):
            for sign in (1, -1) if steps else (1,):
                if steps or flip:
                    to = along(sign * steps) * 2 + (1 - xh if flip else xh)
                    sem = flip if steps == 2 else 2
                    send(cols.at[t], cols.at[t], d_ss.at[0], d_rs.at[sem], (d, to))

    def further(flip):
        landed(cols.at[pl.ds(0, 2)], d_rs.at[flip])
        for held, steps in ((-2 * way, 2 * way), (-2 * way, way), (2 * way, -way)):
            block = along(held) * 2 + (1 - xh if flip else xh)
            to = along(steps) * 2 + xh
            send(cols.at[block], cols.at[block], d_ss.at[1], d_rs.at[3], (d, to))

    further(0)
    landed(rows.at[pl.ds(0, 7)], t_rs.at[0])
    side = d % 2
    block = pl.ds(side * 8, 8)
    sibling = (d + 1 - 2 * side, t)
    half_pick = pick[:, pl.ds(pl.multiple_of(side * 256, 256), 256)]
    half_rows = rows[block].reshape(256, 4 * LANES)
    query_out[...] = lax.dot_general(
        half_pick, half_rows, (((1,), (0,)), ((), ())), preferred_element_type=jnp.float32
    ).astype(jnp.bfloat16)
    send(query_out, query_got, qs_sem.at[0], qs_sem.at[1], sibling)
    send(rows.at[block], rows.at[block], t_ss.at[1], t_rs.at[1], sibling)

    landed(query_got, qs_sem.at[1])
    partial_scores = lax.dot_general(
        query_out[...] + query_got[...],
        rows[place],
        (((1,), (1,)), ((), ())),
        preferred_element_type=jnp.float32,
    )
    for k in range(GROUP):
        score_out[8 * k : 8 * k + 4, 0:32] = partial_scores[4 * k : 4 * k + 4, :]
    for k in sorted(range(1, GROUP), key=lambda k: abs(k - 8)):
        to = lax.rem(t + k, GROUP)
        send(score_out.at[tile(to)], score_got.at[tile(t)], s_ss.at[0], s_rs.at[0], (d, to))
    further(1)
    score_got[tile(t), :] = score_out[tile(t), :]
    landed(rows.at[pl.ds(0, 8)], t_rs.at[1])
    all_rows = rows[...].reshape(GROUP * 32, 4 * LANES)
    turned[...] = lax.dot_general(
        all_rows, swap[...], (((0,), (0,)), ((), ())), preferred_element_type=jnp.float32
    ).astype(jnp.bfloat16)

    landed(cols.at[pl.ds(0, 5)], d_rs.at[2])
    landed(cols.at[pl.ds(0, 6)], d_rs.at[3])
    all_cols = cols[...].reshape(GROUP * 32, 4 * LANES)
    for layer in range(2):
        span = slice(layer * 2 * LANES, (layer + 1) * 2 * LANES)
        result[layer] = jnp.dot(
            turned[span, :], all_cols[:, span], preferred_element_type=jnp.float32
        ) * jnp.float32(1.0 / 512)
        pltpu.make_async_copy(result.at[layer], gram.at[layer], g_sem.at[layer]).start()

    landed(score_got.at[pl.ds(0, 8 * (GROUP - 1))], s_rs.at[0])
    total = score_got[0:8, :]
    for k in range(1, GROUP):
        total = total + score_got[8 * k : 8 * k + 8, :]
    scores[...] = total[0:4, 0:32] / jnp.float32(math.sqrt(2 * RANK * RANK))

    tiles = pl.ds(0, 8 * (GROUP - 1))
    for ref, sem in (
        (a_out, a_ss.at[0]),
        (b_out, b_ss.at[0]),
        (x_out, x_ss.at[0]),
        (land_t.at[tiles], lt_ss.at[0]),
        (land_d.at[tiles], ld_ss.at[0]),
        (rows.at[pl.ds(0, 7)], t_ss.at[0]),
        (rows.at[pl.ds(0, 8)], t_ss.at[1]),
        (cols.at[pl.ds(0, 9)], d_ss.at[0]),
        (cols.at[pl.ds(0, 6)], d_ss.at[1]),
        (score_got.at[tiles], s_ss.at[0]),
        (query_out, qs_sem.at[0]),
        (result.at[0], g_sem.at[0]),
        (result.at[1], g_sem.at[1]),
    ):
        landed(ref, sem)


def local(*args):
    tokens, width = args[0].shape
    query = args[-1].reshape(1, -1)
    dma = pltpu.SemaphoreType.DMA
    f32, bf16, i16 = jnp.float32, jnp.bfloat16, jnp.int16
    vmem = pltpu.VMEM
    scratch = [
        vmem((4, width, tokens), bf16),
        vmem((4, RANK, width), bf16),
        vmem(query.shape, jnp.int32),
        vmem((tokens // SEQ, 2, LANES, SEQ), f32),
        vmem((7, 2, PACK, LANES), i16),
        vmem((7, 2, PACK, LANES), i16),
        vmem((7, PACK, LANES), i16),
        vmem((7, PACK, LANES), i16),
        vmem((RING + 1, PACK, LANES), i16),
        vmem((RING + 1, PACK, LANES), i16),
        vmem((2, RANK, LANES), f32),
        vmem((8 * GROUP, LANES), f32),
        vmem((8 * GROUP, LANES), f32),
        vmem((8 * GROUP, LANES), f32),
        vmem((GROUP, 32, 4 * LANES), bf16),
        vmem((GROUP, 32, 4 * LANES), bf16),
        vmem((GROUP * 32, GROUP * 32), bf16),
        vmem((query.shape[1], GROUP * 32), bf16),
        vmem((4 * LANES, GROUP * 32), bf16),
        vmem((2, 256, 256), f32),
        vmem((query.shape[1], 4 * LANES), bf16),
        vmem((query.shape[1], 4 * LANES), bf16),
        vmem((8 * GROUP, LANES), f32),
        vmem((8 * GROUP, LANES), f32),
        dma((RING, 2)), dma((1,)), dma((1,)),
        dma((1,)), dma((7, 2)),
        dma((1,)), dma((7,)),
        dma((1,)), dma((RING + 1,)),
        dma((1,)), dma((1,)),
        dma((1,)), dma((1,)),
        dma((2,)), dma((2,)),
        dma((2,)), dma((4,)),
        dma((1,)), dma((1,)),
        dma((2,)), dma((2,)),
    ]
    in_hbm = pl.BlockSpec(memory_space=pltpu.HBM)
    in_vmem = pl.BlockSpec(memory_space=pltpu.VMEM)
    return pl.pallas_call(
        kernel,
        out_shape=(
            jax.ShapeDtypeStruct((2, 256, 256), f32),
            jax.ShapeDtypeStruct((4, 32), f32),
        ),
        in_specs=[in_hbm] * 9,
        out_specs=(in_hbm, in_vmem),
        scratch_shapes=scratch,
        compiler_params=pltpu.CompilerParams(
            collective_id=0, has_side_effects=True, vmem_limit_bytes=58 << 20
        ),
    )(*[arg.T for arg in args[:-1]], query)


def solution(mesh):
    in_specs = (
        P("dp", "tensor"),
        P("dp", "tensor"),
        P("dp", "tensor"),
        P("dp", "tensor"),
        P("tensor", None),
        P("tensor", None),
        P("tensor", None),
        P("tensor", None),
        P(),
    )
    out_specs = (P(None, "tensor", "dp"), P("tensor", "dp"))
    return jax.shard_map(local, mesh=mesh, in_specs=in_specs, out_specs=out_specs, check_vma=False)
```

```python
import math

import jax
import jax.numpy as jnp
from jax import lax
from jax.experimental import pallas as pl
from jax.experimental.pallas import tpu as pltpu
from jax.sharding import PartitionSpec as P

SEQ = 128
RANK = 64
GROUP = 16
RING = 8
LANES = 128
PACK = 4 * RANK + 16
MESH = pl.DeviceIdType.MESH
AWAY = (4, -3, 3, -2, 2, -1, 1, 0)


def encode(dst, layers):
    keys = []
    for which, values in enumerate(layers):
        for side in range(2):
            some = values[side * RANK : (side + 1) * RANK]
            top = jnp.max(jnp.abs(some), axis=0, keepdims=True)
            key = jnp.ceil(8.0 * jnp.log2(jnp.maximum(top, 1e-30)) + 0.1)
            scaled = jnp.round(some * jnp.exp2(15.0 - key * 0.125))
            start = (2 * which + side) * RANK
            dst[start : start + RANK, :] = scaled.astype(jnp.int32).astype(jnp.int16)
            keys.append(key)
    row = lax.broadcasted_iota(jnp.int32, (16, SEQ), 0)
    both = jnp.where(row < 4, keys[0], keys[1])
    both = jnp.where(row < 8, both, jnp.where(row < 12, keys[2], keys[3]))
    dst[4 * RANK : PACK, :] = both.astype(jnp.int32).astype(jnp.int16)


def decode(src):
    keys = src[4 * RANK : PACK, :].astype(jnp.int32).astype(jnp.float32)
    out = []
    for which in range(4):
        step = jnp.exp2(keys[4 * which : 4 * which + 1, :] * 0.125 - 15.0)
        whole = src[which * RANK : (which + 1) * RANK, :].astype(jnp.int32).astype(jnp.float32)
        out.append(whole * step)
    return [jnp.concatenate(out[:2], 0), jnp.concatenate(out[2:], 0)]


def add(one, two):
    return [a + b for a, b in zip(one, two)]


def kernel(
    in_one, grad_one, in_two, grad_two, w_in_one, w_out_one, w_in_two, w_out_two, asked,
    gram, scores,
    tok, weights, query, part, a_out, a_got, b_out, b_got, x_out, x_got, square, slices, land_t, land_d,
    rows, cols, swap, pick, turned, result, query_out, query_got, score_out, score_got,
    in_sem, w_sem, q_sem, a_ss, a_rs, b_ss, b_rs, x_ss, x_rs, lt_ss, lt_rs, ld_ss, ld_rs,
    t_ss, t_rs, d_ss, d_rs, s_ss, s_rs, qs_sem, g_sem,
):
    d = lax.axis_index("dp")
    t = lax.axis_index("tensor")
    z, xh = t // 2, t % 2
    way = 1 - 2 * (d % 2)
    owners = [lax.rem(z + way * step + RING, RING) for step in AWAY]
    forward = (d, lax.rem(z + way + RING, RING) * 2 + xh)
    backward = (d, lax.rem(z - way + RING, RING) * 2 + xh)
    partner = (d, z * 2 + 1 - xh)
    def send(src, dst, ss, rs, device):
        pltpu.make_async_remote_copy(
            src_ref=src, dst_ref=dst, send_sem=ss, recv_sem=rs, device_id=device, device_id_type=MESH
        ).start()

    def landed(ref, sem):
        pltpu.make_async_copy(ref, ref, sem).wait()

    def along(steps):
        return lax.rem(z + steps + RING, RING)

    barrier = pltpu.get_barrier_semaphore()
    near = [(d, along(way * steps) * 2 + side) for steps in (1, -1) for side in range(2)]
    near += [partner] + [(lax.rem(d + k, GROUP), t) for k in range(1, GROUP)]

    def greet(devices):
        for device in devices:
            pl.semaphore_signal(barrier, inc=1, device_id=device, device_id_type=MESH)

    def load(i, half):
        start = pl.multiple_of((half * GROUP + 2 * owners[i]) * SEQ, 2 * SEQ)
        for k, source in enumerate((in_one, grad_one, in_two, grad_two)):
            pltpu.make_async_copy(
                source.at[:, pl.ds(start, 2 * SEQ)],
                tok.at[k, :, pl.ds(start, 2 * SEQ)],
                in_sem.at[i, half],
            ).start()

    greet(near[:5])
    for k, weight in enumerate((w_in_one, w_out_one, w_in_two, w_out_two)):
        pltpu.make_async_copy(weight, weights.at[k], w_sem.at[0]).start()
    load(0, 0)
    load(0, 1)
    greet(near[5:])
    landed(weights, w_sem.at[0])

    def project(i, half):
        first = half * GROUP + 2 * owners[i]
        start = pl.multiple_of(first * SEQ, 2 * SEQ)
        landed(tok.at[:, :, pl.ds(start, 2 * SEQ)], in_sem.at[i, half])
        for k in range(4):
            both = jnp.dot(
                weights[k],
                tok[k, :, pl.ds(start, 2 * SEQ)],
                preferred_element_type=jnp.float32,
            )
            span = slice(k % 2 * RANK, (k % 2 + 1) * RANK)
            part[first, k // 2, span, :] = both[:, :SEQ]
            part[first + 1, k // 2, span, :] = both[:, SEQ:]

    def own(half, owner, side):
        index = half * GROUP + 2 * owner + side
        return [part[index, 0], part[index, 1]]

    def ring_a(i):
        for side in (1 - xh, xh):
            total = own(0, owners[i], side)
            if i >= 2:
                landed(a_got.at[i - 2, side], a_rs.at[i - 2, side])
                total = add(total, decode(a_got.at[i - 2, side]))
            encode(a_out.at[i, side], total)
            lane, to = side, forward if i % 2 == 0 else backward
            if i >= 5:
                lane, to = xh, (d, along(way if i % 2 == 0 else -way) * 2 + side)
            send(a_out.at[i, side], a_got.at[i, lane], a_ss.at[0], a_rs.at[i, lane], to)

    def pair(i):
        encode(x_out.at[i], own(1, owners[i], 1 - xh))
        send(x_out.at[i], x_got.at[i], x_ss.at[0], x_rs.at[i], partner)

    def ring_b(i):
        landed(x_got.at[i], x_rs.at[i])
        total = add(own(1, owners[i], xh), decode(x_got.at[i]))
        if i >= 2:
            landed(b_got.at[i - 2], b_rs.at[i - 2])
            total = add(total, decode(b_got.at[i - 2]))
        encode(b_out.at[i], total)
        send(
            b_out.at[i], b_got.at[i], b_ss.at[0], b_rs.at[i], forward if i % 2 == 0 else backward
        )

    def constants():
        at_row = lax.broadcasted_iota(jnp.int32, (GROUP * 32, GROUP * 32), 0)
        at_col = lax.broadcasted_iota(jnp.int32, (GROUP * 32, GROUP * 32), 1)
        mirrored = (at_row % 16) * 32 + (at_row // 16 % 2) * 16 + at_row // 32
        swap[...] = jnp.where(at_col == mirrored, 1.0, 0.0).astype(jnp.bfloat16)
        landed(query, q_sem.at[0])
        row = lax.broadcasted_iota(jnp.int32, pick.shape[::-1], 0)
        example = (row // 32 % 8 * 2 + row // 256) * 32 + row % 32
        pick[...] = jnp.where(example == query[...], 1.0, 0.0).T.astype(jnp.bfloat16)
        score_out[...] = jnp.zeros_like(score_out)

    def first(i):
        project(i, 1)
        pair(i)

    def loads(*which):
        for i, half in which:
            load(i, half)

    project(0, 0)
    pl.semaphore_wait(barrier, len(near))
    ring_a(0)
    first(0)
    loads((1, 0), (1, 1), (2, 1), (3, 1))
    loads((2, 0), (4, 1))
    first(1)
    project(1, 0)
    ring_a(1)
    loads((3, 0), (5, 1))
    first(2)
    loads((4, 0), (6, 1))
    first(3)
    loads((5, 0), (7, 1))
    pltpu.make_async_copy(asked, query, q_sem.at[0]).start()
    project(2, 0)
    ring_b(0)
    for i in range(2, RING - 1):
        ring_a(i)
        ring_b(i - 1)
        if i == 2:
            loads((6, 0), (7, 0))
        if i + 2 < RING:
            first(i + 2)
        if i < RING - 2:
            project(i + 1, 0)
        if i == RING - 3:
            project(RING - 1, 0)
            encode(x_out.at[RING], own(0, z, 1 - xh))
            send(x_out.at[RING], x_got.at[RING], x_ss.at[0], x_rs.at[RING], partner)
    ring_b(RING - 2)
    constants()

    def features(half, sums):
        for layer in range(2):
            outer = lax.dot_general(
                sums[layer][RANK:], sums[layer], (((1,), (1,)), ((), ())),
                precision=lax.Precision.HIGHEST, preferred_element_type=jnp.float32,
            )
            scaled = outer / jnp.float32(math.sqrt(SEQ))
            square[layer] = scaled.astype(jnp.bfloat16).astype(jnp.float32)
        for layer in range(2):
            for pair_of in range(2):
                even = square[layer, pl.ds(2 * pair_of, GROUP, stride=4), :]
                odd = square[layer, pl.ds(2 * pair_of + 1, GROUP, stride=4), :]
                slices[pl.ds(half * 4 + layer * 2 + pair_of, GROUP, stride=8), :] = jnp.concatenate(
                    [even[:, :RANK], odd[:, :RANK]], 1
                )

    for i in (5, 6):
        landed(b_got.at[i], b_rs.at[i])
    landed(x_got.at[RING - 1], x_rs.at[RING - 1])
    total = add(own(1, z, xh), decode(x_got.at[RING - 1]))
    for i in (5, 6):
        total = add(total, decode(b_got.at[i]))
    features(1, total)
    landed(x_got.at[RING], x_rs.at[RING])
    total = add(own(0, z, xh), decode(x_got.at[RING]))
    for i in (5, 6):
        for side in range(2):
            landed(a_got.at[i, side], a_rs.at[i, side])
            total = add(total, decode(a_got.at[i, side]))
    features(0, total)

    place = d % 2 * 8 + d // 2

    def tile(index):
        return pl.ds(pl.multiple_of(8 * index, 8), 8)

    for k in sorted(range(1, GROUP), key=lambda k: abs(k - 8)):
        to = lax.rem(t + k, GROUP)
        send(slices.at[tile(to)], land_t.at[tile(t)], lt_ss.at[0], lt_rs.at[0], (d, to))
    for k in range(1, GROUP):
        to = lax.rem(d + k, GROUP)
        send(slices.at[tile(to)], land_d.at[tile(place)], ld_ss.at[0], ld_rs.at[0], (to, t))
    land_t[tile(t), :] = slices[tile(t), :]
    land_d[tile(place), :] = slices[tile(d), :]

    def gather(land, block, rs):
        landed(land.at[pl.ds(0, 8 * (GROUP - 1))], rs.at[0])
        for half in range(2):
            lanes = [land[pl.ds(half * 4 + k, GROUP, stride=8), :] for k in range(4)]
            block[half * GROUP : (half + 1) * GROUP, :] = jnp.concatenate(lanes, 1).astype(
                jnp.bfloat16
            )

    gather(land_t, rows.at[place], lt_rs)
    for k in range(1, 8):
        send(rows.at[place], rows.at[place], t_ss.at[0], t_rs.at[0], (lax.rem(d + 2 * k, GROUP), t))

    gather(land_d, cols.at[t], ld_rs)
    for flip in range(2):
        for steps in (2, 1, 0):
            for sign in (1, -1) if steps else (1,):
                if steps or flip:
                    to = along(sign * steps) * 2 + (1 - xh if flip else xh)
                    sem = flip if steps == 2 else 2
                    send(cols.at[t], cols.at[t], d_ss.at[0], d_rs.at[sem], (d, to))

    def further(flip):
        landed(cols.at[pl.ds(0, 2)], d_rs.at[flip])
        for held, steps in ((-2 * way, 2 * way), (-2 * way, way), (2 * way, -way)):
            block = along(held) * 2 + (1 - xh if flip else xh)
            to = along(steps) * 2 + xh
            send(cols.at[block], cols.at[block], d_ss.at[1], d_rs.at[3], (d, to))

    further(0)
    landed(rows.at[pl.ds(0, 7)], t_rs.at[0])
    side = d % 2
    block = pl.ds(side * 8, 8)
    sibling = (d + 1 - 2 * side, t)
    half_pick = pick[:, pl.ds(pl.multiple_of(side * 256, 256), 256)]
    half_rows = rows[block].reshape(256, 4 * LANES)
    query_out[...] = lax.dot_general(
        half_pick, half_rows, (((1,), (0,)), ((), ())), preferred_element_type=jnp.float32
    ).astype(jnp.bfloat16)
    send(query_out, query_got, qs_sem.at[0], qs_sem.at[1], sibling)
    send(rows.at[block], rows.at[block], t_ss.at[1], t_rs.at[1], sibling)

    landed(query_got, qs_sem.at[1])
    partial_scores = lax.dot_general(
        query_out[...] + query_got[...],
        rows[place],
        (((1,), (1,)), ((), ())),
        preferred_element_type=jnp.float32,
    )
    for k in range(GROUP):
        score_out[8 * k : 8 * k + 4, 0:32] = partial_scores[4 * k : 4 * k + 4, :]
    for k in sorted(range(1, GROUP), key=lambda k: abs(k - 8)):
        to = lax.rem(t + k, GROUP)
        send(score_out.at[tile(to)], score_got.at[tile(t)], s_ss.at[0], s_rs.at[0], (d, to))
    further(1)
    score_got[tile(t), :] = score_out[tile(t), :]
    landed(rows.at[pl.ds(0, 8)], t_rs.at[1])
    all_rows = rows[...].reshape(GROUP * 32, 4 * LANES)
    turned[...] = lax.dot_general(
        all_rows, swap[...], (((0,), (0,)), ((), ())), preferred_element_type=jnp.float32
    ).astype(jnp.bfloat16)

    landed(cols.at[pl.ds(0, 5)], d_rs.at[2])
    landed(cols.at[pl.ds(0, 6)], d_rs.at[3])
    all_cols = cols[...].reshape(GROUP * 32, 4 * LANES)
    for layer in range(2):
        span = slice(layer * 2 * LANES, (layer + 1) * 2 * LANES)
        result[layer] = jnp.dot(
            turned[span, :], all_cols[:, span], preferred_element_type=jnp.float32
        ) * jnp.float32(1.0 / 512)
        pltpu.make_async_copy(result.at[layer], gram.at[layer], g_sem.at[layer]).start()

    landed(score_got.at[pl.ds(0, 8 * (GROUP - 1))], s_rs.at[0])
    total = score_got[0:8, :]
    for k in range(1, GROUP):
        total = total + score_got[8 * k : 8 * k + 8, :]
    scores[...] = total[0:4, 0:32] / jnp.float32(math.sqrt(2 * RANK * RANK))

    tiles = pl.ds(0, 8 * (GROUP - 1))
    for ref, sem in (
        (a_out, a_ss.at[0]),
        (b_out, b_ss.at[0]),
        (x_out, x_ss.at[0]),
        (land_t.at[tiles], lt_ss.at[0]),
        (land_d.at[tiles], ld_ss.at[0]),
        (rows.at[pl.ds(0, 7)], t_ss.at[0]),
        (rows.at[pl.ds(0, 8)], t_ss.at[1]),
        (cols.at[pl.ds(0, 9)], d_ss.at[0]),
        (cols.at[pl.ds(0, 6)], d_ss.at[1]),
        (score_got.at[tiles], s_ss.at[0]),
        (query_out, qs_sem.at[0]),
        (result.at[0], g_sem.at[0]),
        (result.at[1], g_sem.at[1]),
    ):
        landed(ref, sem)


def local(*args):
    tokens, width = args[0].shape
    query = args[-1].reshape(1, -1)
    dma = pltpu.SemaphoreType.DMA
    f32, bf16, i16 = jnp.float32, jnp.bfloat16, jnp.int16
    vmem = pltpu.VMEM
    scratch = [
        vmem((4, width, tokens), bf16),
        vmem((4, RANK, width), bf16),
        vmem(query.shape, jnp.int32),
        vmem((tokens // SEQ, 2, LANES, SEQ), f32),
        vmem((7, 2, PACK, LANES), i16),
        vmem((7, 2, PACK, LANES), i16),
        vmem((7, PACK, LANES), i16),
        vmem((7, PACK, LANES), i16),
        vmem((RING + 1, PACK, LANES), i16),
        vmem((RING + 1, PACK, LANES), i16),
        vmem((2, RANK, LANES), f32),
        vmem((8 * GROUP, LANES), f32),
        vmem((8 * GROUP, LANES), f32),
        vmem((8 * GROUP, LANES), f32),
        vmem((GROUP, 32, 4 * LANES), bf16),
        vmem((GROUP, 32, 4 * LANES), bf16),
        vmem((GROUP * 32, GROUP * 32), bf16),
        vmem((query.shape[1], GROUP * 32), bf16),
        vmem((4 * LANES, GROUP * 32), bf16),
        vmem((2, 256, 256), f32),
        vmem((query.shape[1], 4 * LANES), bf16),
        vmem((query.shape[1], 4 * LANES), bf16),
        vmem((8 * GROUP, LANES), f32),
        vmem((8 * GROUP, LANES), f32),
        dma((RING, 2)), dma((1,)), dma((1,)),
        dma((1,)), dma((7, 2)),
        dma((1,)), dma((7,)),
        dma((1,)), dma((RING + 1,)),
        dma((1,)), dma((1,)),
        dma((1,)), dma((1,)),
        dma((2,)), dma((2,)),
        dma((2,)), dma((4,)),
        dma((1,)), dma((1,)),
        dma((2,)), dma((2,)),
    ]
    in_hbm = pl.BlockSpec(memory_space=pltpu.HBM)
    in_vmem = pl.BlockSpec(memory_space=pltpu.VMEM)
    return pl.pallas_call(
        kernel,
        out_shape=(
            jax.ShapeDtypeStruct((2, 256, 256), f32),
            jax.ShapeDtypeStruct((4, 32), f32),
        ),
        in_specs=[in_hbm] * 9,
        out_specs=(in_hbm, in_vmem),
        scratch_shapes=scratch,
        compiler_params=pltpu.CompilerParams(
            collective_id=0, has_side_effects=True, vmem_limit_bytes=58 << 20
        ),
    )(*[arg.T for arg in args[:-1]], query)


def solution(mesh):
    in_specs = (
        P("dp", "tensor"),
        P("dp", "tensor"),
        P("dp", "tensor"),
        P("dp", "tensor"),
        P("tensor", None),
        P("tensor", None),
        P("tensor", None),
        P("tensor", None),
        P(),
    )
    out_specs = (P(None, "tensor", "dp"), P("tensor", "dp"))
    return jax.shard_map(local, mesh=mesh, in_specs=in_specs, out_specs=out_specs, check_vma=False)
```

```python
import math

import jax
import jax.numpy as jnp
from jax import lax
from jax.experimental import pallas as pl
from jax.experimental.pallas import tpu as pltpu
from jax.sharding import PartitionSpec as P

SEQ = 128
RANK = 64
GROUP = 16
RING = 8
LANES = 128
PACK = 4 * RANK + 16
MESH = pl.DeviceIdType.MESH
AWAY = (4, -3, 3, -2, 2, -1, 1, 0)


def encode(dst, layers):
    keys = []
    for which, values in enumerate(layers):
        for side in range(2):
            some = values[side * RANK : (side + 1) * RANK]
            top = jnp.max(jnp.abs(some), axis=0, keepdims=True)
            key = jnp.ceil(8.0 * jnp.log2(jnp.maximum(top, 1e-30)) + 0.1)
            scaled = jnp.round(some * jnp.exp2(15.0 - key * 0.125))
            start = (2 * which + side) * RANK
            dst[start : start + RANK, :] = scaled.astype(jnp.int32).astype(jnp.int16)
            keys.append(key)
    row = lax.broadcasted_iota(jnp.int32, (16, SEQ), 0)
    both = jnp.where(row < 4, keys[0], keys[1])
    both = jnp.where(row < 8, both, jnp.where(row < 12, keys[2], keys[3]))
    dst[4 * RANK : PACK, :] = both.astype(jnp.int32).astype(jnp.int16)


def decode(src):
    keys = src[4 * RANK : PACK, :].astype(jnp.int32).astype(jnp.float32)
    out = []
    for which in range(4):
        step = jnp.exp2(keys[4 * which : 4 * which + 1, :] * 0.125 - 15.0)
        whole = src[which * RANK : (which + 1) * RANK, :].astype(jnp.int32).astype(jnp.float32)
        out.append(whole * step)
    return [jnp.concatenate(out[:2], 0), jnp.concatenate(out[2:], 0)]


def add(one, two):
    return [a + b for a, b in zip(one, two)]


def kernel(
    in_one, grad_one, in_two, grad_two, w_in_one, w_out_one, w_in_two, w_out_two, asked,
    gram, scores,
    tok, weights, query, part, a_out, a_got, b_out, b_got, x_out, x_got, square, slices, land_t, land_d,
    rows, cols, swap, pick, turned, result, query_out, query_got, score_out, score_got,
    in_sem, w_sem, q_sem, a_ss, a_rs, b_ss, b_rs, x_ss, x_rs, lt_ss, lt_rs, ld_ss, ld_rs,
    t_ss, t_rs, d_ss, d_rs, s_ss, s_rs, qs_sem, g_sem,
):
    d = lax.axis_index("dp")
    t = lax.axis_index("tensor")
    z, xh = t // 2, t % 2
    way = 1 - 2 * (d % 2)
    owners = [lax.rem(z + way * step + RING, RING) for step in AWAY]
    forward = (d, lax.rem(z + way + RING, RING) * 2 + xh)
    backward = (d, lax.rem(z - way + RING, RING) * 2 + xh)
    partner = (d, z * 2 + 1 - xh)
    def send(src, dst, ss, rs, device):
        pltpu.make_async_remote_copy(
            src_ref=src, dst_ref=dst, send_sem=ss, recv_sem=rs, device_id=device, device_id_type=MESH
        ).start()

    def landed(ref, sem):
        pltpu.make_async_copy(ref, ref, sem).wait()

    def along(steps):
        return lax.rem(z + steps + RING, RING)

    barrier = pltpu.get_barrier_semaphore()
    near = [(d, along(way * steps) * 2 + side) for steps in (1, -1) for side in range(2)]
    near += [partner] + [(lax.rem(d + k, GROUP), t) for k in range(1, GROUP)]

    def greet(devices):
        for device in devices:
            pl.semaphore_signal(barrier, inc=1, device_id=device, device_id_type=MESH)

    def load(i, half):
        start = pl.multiple_of((half * GROUP + 2 * owners[i]) * SEQ, 2 * SEQ)
        for k, source in enumerate((in_one, grad_one, in_two, grad_two)):
            pltpu.make_async_copy(
                source.at[:, pl.ds(start, 2 * SEQ)],
                tok.at[k, :, pl.ds(start, 2 * SEQ)],
                in_sem.at[i, half],
            ).start()

    greet(near[:5])
    for k, weight in enumerate((w_in_one, w_out_one, w_in_two, w_out_two)):
        pltpu.make_async_copy(weight, weights.at[k], w_sem.at[0]).start()
    load(0, 0)
    load(0, 1)
    greet(near[5:])
    landed(weights, w_sem.at[0])

    def project(i, half):
        first = half * GROUP + 2 * owners[i]
        start = pl.multiple_of(first * SEQ, 2 * SEQ)
        landed(tok.at[:, :, pl.ds(start, 2 * SEQ)], in_sem.at[i, half])
        for k in range(4):
            both = jnp.dot(
                weights[k],
                tok[k, :, pl.ds(start, 2 * SEQ)],
                preferred_element_type=jnp.float32,
            )
            span = slice(k % 2 * RANK, (k % 2 + 1) * RANK)
            part[first, k // 2, span, :] = both[:, :SEQ]
            part[first + 1, k // 2, span, :] = both[:, SEQ:]

    def own(half, owner, side):
        index = half * GROUP + 2 * owner + side
        return [part[index, 0], part[index, 1]]

    def ring_a(i):
        for side in range(2):
            total = own(0, owners[i], side)
            if i >= 2:
                landed(a_got.at[i - 2, side], a_rs.at[i - 2, side])
                total = add(total, decode(a_got.at[i - 2, side]))
            encode(a_out.at[i, side], total)
            lane, to = side, forward if i % 2 == 0 else backward
            if i >= 5:
                lane, to = xh, (d, along(way if i % 2 == 0 else -way) * 2 + side)
            send(a_out.at[i, side], a_got.at[i, lane], a_ss.at[0], a_rs.at[i, lane], to)

    def pair(i):
        encode(x_out.at[i], own(1, owners[i], 1 - xh))
        send(x_out.at[i], x_got.at[i], x_ss.at[0], x_rs.at[i], partner)

    def ring_b(i):
        landed(x_got.at[i], x_rs.at[i])
        total = add(own(1, owners[i], xh), decode(x_got.at[i]))
        if i >= 2:
            landed(b_got.at[i - 2], b_rs.at[i - 2])
            total = add(total, decode(b_got.at[i - 2]))
        encode(b_out.at[i], total)
        send(
            b_out.at[i], b_got.at[i], b_ss.at[0], b_rs.at[i], forward if i % 2 == 0 else backward
        )

    def constants():
        at_row = lax.broadcasted_iota(jnp.int32, (GROUP * 32, GROUP * 32), 0)
        at_col = lax.broadcasted_iota(jnp.int32, (GROUP * 32, GROUP * 32), 1)
        mirrored = (at_row % 16) * 32 + (at_row // 16 % 2) * 16 + at_row // 32
        swap[...] = jnp.where(at_col == mirrored, 1.0, 0.0).astype(jnp.bfloat16)
        landed(query, q_sem.at[0])
        row = lax.broadcasted_iota(jnp.int32, pick.shape[::-1], 0)
        example = (row // 32 % 8 * 2 + row // 256) * 32 + row % 32
        pick[...] = jnp.where(example == query[...], 1.0, 0.0).T.astype(jnp.bfloat16)
        score_out[...] = jnp.zeros_like(score_out)

    def first(i):
        project(i, 1)
        pair(i)

    def loads(*which):
        for i, half in which:
            load(i, half)

    project(0, 0)
    pl.semaphore_wait(barrier, len(near))
    ring_a(0)
    first(0)
    loads((1, 0), (1, 1), (2, 1), (3, 1))
    loads((2, 0), (4, 1))
    first(1)
    project(1, 0)
    ring_a(1)
    loads((3, 0), (5, 1))
    first(2)
    loads((4, 0), (6, 1))
    first(3)
    loads((5, 0), (7, 1))
    pltpu.make_async_copy(asked, query, q_sem.at[0]).start()
    project(2, 0)
    ring_b(0)
    for i in range(2, RING - 1):
        ring_a(i)
        ring_b(i - 1)
        if i == 2:
            loads((6, 0), (7, 0))
        if i + 2 < RING:
            first(i + 2)
        if i < RING - 2:
            project(i + 1, 0)
        if i == RING - 3:
            project(RING - 1, 0)
            encode(x_out.at[RING], own(0, z, 1 - xh))
            send(x_out.at[RING], x_got.at[RING], x_ss.at[0], x_rs.at[RING], partner)
    ring_b(RING - 2)
    constants()

    def features(half, sums):
        for layer in range(2):
            outer = lax.dot_general(
                sums[layer][RANK:], sums[layer], (((1,), (1,)), ((), ())),
                precision=lax.Precision.HIGHEST, preferred_element_type=jnp.float32,
            )
            scaled = outer / jnp.float32(math.sqrt(SEQ))
            square[layer] = scaled.astype(jnp.bfloat16).astype(jnp.float32)
        for layer in range(2):
            for pair_of in range(2):
                even = square[layer, pl.ds(2 * pair_of, GROUP, stride=4), :]
                odd = square[layer, pl.ds(2 * pair_of + 1, GROUP, stride=4), :]
                slices[pl.ds(half * 4 + layer * 2 + pair_of, GROUP, stride=8), :] = jnp.concatenate(
                    [even[:, :RANK], odd[:, :RANK]], 1
                )

    landed(x_got.at[RING], x_rs.at[RING])
    total = add(own(0, z, xh), decode(x_got.at[RING]))
    for i in (5, 6):
        for side in range(2):
            landed(a_got.at[i, side], a_rs.at[i, side])
            total = add(total, decode(a_got.at[i, side]))
    features(0, total)
    for i in (5, 6):
        landed(b_got.at[i], b_rs.at[i])
    landed(x_got.at[RING - 1], x_rs.at[RING - 1])
    total = add(own(1, z, xh), decode(x_got.at[RING - 1]))
    for i in (5, 6):
        total = add(total, decode(b_got.at[i]))
    features(1, total)

    place = d % 2 * 8 + d // 2

    def tile(index):
        return pl.ds(pl.multiple_of(8 * index, 8), 8)

    for k in sorted(range(1, GROUP), key=lambda k: abs(k - 8)):
        to = lax.rem(t + k, GROUP)
        send(slices.at[tile(to)], land_t.at[tile(t)], lt_ss.at[0], lt_rs.at[0], (d, to))
    for k in range(1, GROUP):
        to = lax.rem(d + k, GROUP)
        send(slices.at[tile(to)], land_d.at[tile(place)], ld_ss.at[0], ld_rs.at[0], (to, t))
    land_t[tile(t), :] = slices[tile(t), :]
    land_d[tile(place), :] = slices[tile(d), :]

    def gather(land, block, rs):
        landed(land.at[pl.ds(0, 8 * (GROUP - 1))], rs.at[0])
        for half in range(2):
            lanes = [land[pl.ds(half * 4 + k, GROUP, stride=8), :] for k in range(4)]
            block[half * GROUP : (half + 1) * GROUP, :] = jnp.concatenate(lanes, 1).astype(
                jnp.bfloat16
            )

    gather(land_t, rows.at[place], lt_rs)
    for k in range(1, 8):
        send(rows.at[place], rows.at[place], t_ss.at[0], t_rs.at[0], (lax.rem(d + 2 * k, GROUP), t))

    gather(land_d, cols.at[t], ld_rs)
    for flip in range(2):
        for steps in (2, 1, 0):
            for sign in (1, -1) if steps else (1,):
                if steps or flip:
                    to = along(sign * steps) * 2 + (1 - xh if flip else xh)
                    sem = flip if steps == 2 else 2
                    send(cols.at[t], cols.at[t], d_ss.at[0], d_rs.at[sem], (d, to))

    def further(flip):
        landed(cols.at[pl.ds(0, 2)], d_rs.at[flip])
        for held, steps in ((-2 * way, 2 * way), (-2 * way, way), (2 * way, -way)):
            block = along(held) * 2 + (1 - xh if flip else xh)
            to = along(steps) * 2 + xh
            send(cols.at[block], cols.at[block], d_ss.at[1], d_rs.at[3], (d, to))

    further(0)
    landed(rows.at[pl.ds(0, 7)], t_rs.at[0])
    side = d % 2
    block = pl.ds(side * 8, 8)
    sibling = (d + 1 - 2 * side, t)
    half_pick = pick[:, pl.ds(pl.multiple_of(side * 256, 256), 256)]
    half_rows = rows[block].reshape(256, 4 * LANES)
    query_out[...] = lax.dot_general(
        half_pick, half_rows, (((1,), (0,)), ((), ())), preferred_element_type=jnp.float32
    ).astype(jnp.bfloat16)
    send(query_out, query_got, qs_sem.at[0], qs_sem.at[1], sibling)
    send(rows.at[block], rows.at[block], t_ss.at[1], t_rs.at[1], sibling)

    landed(query_got, qs_sem.at[1])
    partial_scores = lax.dot_general(
        query_out[...] + query_got[...],
        rows[place],
        (((1,), (1,)), ((), ())),
        preferred_element_type=jnp.float32,
    )
    for k in range(GROUP):
        score_out[8 * k : 8 * k + 4, 0:32] = partial_scores[4 * k : 4 * k + 4, :]
    for k in sorted(range(1, GROUP), key=lambda k: abs(k - 8)):
        to = lax.rem(t + k, GROUP)
        send(score_out.at[tile(to)], score_got.at[tile(t)], s_ss.at[0], s_rs.at[0], (d, to))
    further(1)
    score_got[tile(t), :] = score_out[tile(t), :]
    landed(rows.at[pl.ds(0, 8)], t_rs.at[1])
    all_rows = rows[...].reshape(GROUP * 32, 4 * LANES)
    turned[...] = lax.dot_general(
        all_rows, swap[...], (((0,), (0,)), ((), ())), preferred_element_type=jnp.float32
    ).astype(jnp.bfloat16)

    landed(cols.at[pl.ds(0, 5)], d_rs.at[2])
    landed(cols.at[pl.ds(0, 6)], d_rs.at[3])
    all_cols = cols[...].reshape(GROUP * 32, 4 * LANES)
    for layer in range(2):
        span = slice(layer * 2 * LANES, (layer + 1) * 2 * LANES)
        result[layer] = jnp.dot(
            turned[span, :], all_cols[:, span], preferred_element_type=jnp.float32
        ) * jnp.float32(1.0 / 512)
        pltpu.make_async_copy(result.at[layer], gram.at[layer], g_sem.at[layer]).start()

    landed(score_got.at[pl.ds(0, 8 * (GROUP - 1))], s_rs.at[0])
    total = score_got[0:8, :]
    for k in range(1, GROUP):
        total = total + score_got[8 * k : 8 * k + 8, :]
    scores[...] = total[0:4, 0:32] / jnp.float32(math.sqrt(2 * RANK * RANK))

    tiles = pl.ds(0, 8 * (GROUP - 1))
    for ref, sem in (
        (a_out, a_ss.at[0]),
        (b_out, b_ss.at[0]),
        (x_out, x_ss.at[0]),
        (land_t.at[tiles], lt_ss.at[0]),
        (land_d.at[tiles], ld_ss.at[0]),
        (rows.at[pl.ds(0, 7)], t_ss.at[0]),
        (rows.at[pl.ds(0, 8)], t_ss.at[1]),
        (cols.at[pl.ds(0, 9)], d_ss.at[0]),
        (cols.at[pl.ds(0, 6)], d_ss.at[1]),
        (score_got.at[tiles], s_ss.at[0]),
        (query_out, qs_sem.at[0]),
        (result.at[0], g_sem.at[0]),
        (result.at[1], g_sem.at[1]),
    ):
        landed(ref, sem)


def local(*args):
    tokens, width = args[0].shape
    query = args[-1].reshape(1, -1)
    dma = pltpu.SemaphoreType.DMA
    f32, bf16, i16 = jnp.float32, jnp.bfloat16, jnp.int16
    vmem = pltpu.VMEM
    scratch = [
        vmem((4, width, tokens), bf16),
        vmem((4, RANK, width), bf16),
        vmem(query.shape, jnp.int32),
        vmem((tokens // SEQ, 2, LANES, SEQ), f32),
        vmem((7, 2, PACK, LANES), i16),
        vmem((7, 2, PACK, LANES), i16),
        vmem((7, PACK, LANES), i16),
        vmem((7, PACK, LANES), i16),
        vmem((RING + 1, PACK, LANES), i16),
        vmem((RING + 1, PACK, LANES), i16),
        vmem((2, RANK, LANES), f32),
        vmem((8 * GROUP, LANES), f32),
        vmem((8 * GROUP, LANES), f32),
        vmem((8 * GROUP, LANES), f32),
        vmem((GROUP, 32, 4 * LANES), bf16),
        vmem((GROUP, 32, 4 * LANES), bf16),
        vmem((GROUP * 32, GROUP * 32), bf16),
        vmem((query.shape[1], GROUP * 32), bf16),
        vmem((4 * LANES, GROUP * 32), bf16),
        vmem((2, 256, 256), f32),
        vmem((query.shape[1], 4 * LANES), bf16),
        vmem((query.shape[1], 4 * LANES), bf16),
        vmem((8 * GROUP, LANES), f32),
        vmem((8 * GROUP, LANES), f32),
        dma((RING, 2)), dma((1,)), dma((1,)),
        dma((1,)), dma((7, 2)),
        dma((1,)), dma((7,)),
        dma((1,)), dma((RING + 1,)),
        dma((1,)), dma((1,)),
        dma((1,)), dma((1,)),
        dma((2,)), dma((2,)),
        dma((2,)), dma((4,)),
        dma((1,)), dma((1,)),
        dma((2,)), dma((2,)),
    ]
    in_hbm = pl.BlockSpec(memory_space=pltpu.HBM)
    in_vmem = pl.BlockSpec(memory_space=pltpu.VMEM)
    return pl.pallas_call(
        kernel,
        out_shape=(
            jax.ShapeDtypeStruct((2, 256, 256), f32),
            jax.ShapeDtypeStruct((4, 32), f32),
        ),
        in_specs=[in_hbm] * 9,
        out_specs=(in_hbm, in_vmem),
        scratch_shapes=scratch,
        compiler_params=pltpu.CompilerParams(
            collective_id=0, has_side_effects=True, vmem_limit_bytes=58 << 20
        ),
    )(*[arg.T for arg in args[:-1]], query)


def solution(mesh):
    in_specs = (
        P("dp", "tensor"),
        P("dp", "tensor"),
        P("dp", "tensor"),
        P("dp", "tensor"),
        P("tensor", None),
        P("tensor", None),
        P("tensor", None),
        P("tensor", None),
        P(),
    )
    out_specs = (P(None, "tensor", "dp"), P("tensor", "dp"))
    return jax.shard_map(local, mesh=mesh, in_specs=in_specs, out_specs=out_specs, check_vma=False)
```
